512 devices in a mesh: row: 16 (over x_lo, z), col: 32 (over y, x_hi, core).
Axes of the slice: x: 4 (x_hi: 2, x_lo: 2; x = x_hi * 2 + x_lo), y: 8, z: 8, core: 2. Of those that a mesh axis runs over, the one named last changes fastest.
Arguments:
- covariance: float32 [16384, 16384], P('row', 'col')
- rotations: float32 [2, 64, 256, 256], P(None, 'row', 'col')
- pairing: int32 [2, 128], replicated, may hold values from 0 to 127, as said below
Outputs:
- transformed: float32 [16384, 16384], P('row', 'col')
The draws below stay inside these ranges and needn't reach their ends.
Inputs may be any that keep to these rules, and one draw needn't show every extreme that they name: `pairing`: each row is its own inverse and moves entries by at most one: positions 2k + 1 and 2k + 2 either trade places or stay, and every such pair with 2k + 2 a multiple of 4 trades places.
All inputs are finite; a program needn't handle non-finite values.
Results may differ from the reference program's by a relative error of at most 0.00015.
Values sent between devices are 32-bit elements; how exact they have to be, the bound alone decides.
A program may use at most 64 MiB of HBM per device.

```python
import jax
import jax.numpy as jnp
from jax import lax

ORDER = 16384
BLOCK = 128
ROUNDS = 2
NB = 128
PAIRS = 64
COLBLK = 4


def draw_covariance(key, part):
    key = jax.random.fold_in(key, 11)
    noise = jax.random.normal(key, (ORDER, ORDER), jnp.float32)
    symmetric = (noise + noise.T) * 0.5
    rows = lax_iota(ORDER)
    diag = jnp.where(rows[:, None] == rows[None, :], 2.0, 0.0).astype(jnp.float32)
    return symmetric + diag


def lax_iota(count):
    return jnp.arange(count, dtype=jnp.int32)


def draw_rotations(key, part):
    key = jax.random.fold_in(key, 23)
    shape = (ROUNDS, PAIRS, 2 * BLOCK, 2 * BLOCK)
    noise = jax.random.normal(key, shape, jnp.float32)
    index = lax_iota(2 * BLOCK)
    ident = jnp.where(index[:, None] == index[None, :], 1.0, 0.0).astype(jnp.float32)
    return ident + noise * (0.4 / (2.0 * BLOCK) ** 0.5)


def draw_pairing(key, part):
    key = jax.random.fold_in(key, 37)
    coins = jax.random.randint(key, (ROUNDS, NB), 0, 2)
    place = lax_iota(NB)[None, :]
    flag = (coins == 1) | ((place + 1) % COLBLK == 0)
    flag = flag & (place % 2 == 1) & (place + 1 < NB)
    flag_num = flag.astype(jnp.int32)
    before = jnp.concatenate([jnp.zeros((ROUNDS, 1), jnp.int32), flag_num[:, :-1]], axis=1)
    return (place + flag_num - before).astype(jnp.int32)


def setup_inputs(seed: int = 0) -> dict:
    arg_keys = jax.random.split(jax.random.key(seed), 4)
    return {
        "covariance": draw_covariance(jax.random.fold_in(arg_keys[3], 71), 0),
        "rotations": draw_rotations(jax.random.fold_in(arg_keys[3], 71), 0),
        "pairing": draw_pairing(jax.random.fold_in(arg_keys[3], 71), 0),
    }


def reference(covariance, rotations, pairing):
    current = covariance
    for rnd in range(ROUNDS):
        rot = rotations[rnd]
        left = current.reshape(PAIRS, 2 * BLOCK, ORDER)
        left = jnp.einsum("kio,kic->koc", rot, left, precision=lax.Precision.HIGHEST).reshape(ORDER, ORDER)
        both = left.reshape(ORDER, PAIRS, 2 * BLOCK)
        both = jnp.einsum("rki,kio->rko", both, rot, precision=lax.Precision.HIGHEST).reshape(ORDER, ORDER)
        order_now = pairing[rnd].astype(jnp.int32)
        blocks = both.reshape(NB, BLOCK, NB, BLOCK)
        blocks = jnp.take(blocks, order_now, axis=0)
        blocks = jnp.take(blocks, order_now, axis=2)
        current = blocks.reshape(ORDER, ORDER)
    return current
```

```python
import jax
import jax.numpy as jnp
from jax import lax
from jax.experimental import pallas as pl
from jax.experimental.pallas import tpu as pltpu
from jax.sharding import PartitionSpec as P

BLOCK = 128
PAIR = 2 * BLOCK
ROWS, COLS = 16, 32
XL, Z, Y, XH, CORE = 2, 8, 8, 2, 2
RB, CB = 8, 4
RP = RB // 2
MESH = pl.DeviceIdType.MESH
F32, B16 = jnp.float32, jnp.bfloat16


def split(value):
    high = value.astype(B16)
    low = (value - high.astype(F32)).astype(B16)
    return high, low


def dot(a, b):
    return jnp.dot(a, b, preferred_element_type=F32)


def dot3(a, b):
    return dot(a[0], b[0]) + (dot(a[0], b[1]) + dot(a[1], b[0]))


def kernel(
    cov_ref, rot_ref, pair_ref, out_ref,
    cbuf, rr, rc, rrt, rcs, xs, xr, wmid, v, vr, u, ur, ts, tr, tmid, obuf,
    loc_sem, tr_s, tr_r, xl_s, xl_r, xh_s, xh_r, z_s, z_r, y_s, y_r, mt_s, mt_r,
    cx_s, cx_r, vx_s, vx_r, ux_s, ux_r, tx_s, tx_r, out_sem,
):
    r = lax.axis_index("row")
    c = lax.axis_index("col")
    xl, z = r // Z, r % Z
    y, xh, core = c // 4, (c // 2) % 2, c % 2

    def dev(row, col):
        return (row, col)

    mate = dev(r, y * 4 + xh * 2 + (1 - core))
    xh_mate = dev(r, y * 4 + (1 - xh) * 2 + core)
    y_next = dev(r, ((y + 1) % Y) * 4 + xh * 2 + core)
    y_prev = dev(r, ((y + Y - 1) % Y) * 4 + xh * 2 + core)
    xl_mate = dev((1 - xl) * Z + z, c)
    z_next = dev(xl * Z + (z + 1) % Z, c)
    z_prev = dev(xl * Z + (z + Z - 1) % Z, c)
    up = dev((r + ROWS - 1) % ROWS, c)
    down = dev((r + 1) % ROWS, c)
    left = dev(r, (c + COLS - 1) % COLS)
    right = dev(r, (c + 1) % COLS)
    across = [dev(c // 2, 2 * r + h) for h in range(2)]
    stays = [jnp.logical_and(c // 2 == r, core == h) for h in range(2)]
    has_up, has_down = r > 0, r < ROWS - 1
    has_left, has_right = c > 0, c < COLS - 1

    def remote(src, dst, send, recv, device):
        return pltpu.make_async_remote_copy(
            src_ref=src, dst_ref=dst, send_sem=send, recv_sem=recv,
            device_id=device, device_id_type=MESH,
        )

    started = []

    def go(copy):
        copy.start()
        started.append(copy)

    load = pltpu.make_async_copy(cov_ref, cbuf, loc_sem.at[0])
    load.start()
    own = [
        pltpu.make_async_copy(rot_ref.at[t], rr.at[t, :, y, xh, core], loc_sem.at[1 + t])
        for t in range(2)
    ]
    for t in range(2):
        own[t].start()

    barrier = pltpu.get_barrier_semaphore()
    peers = [mate, xh_mate, y_next, y_prev, xl_mate, z_next, z_prev, up, down, left, right]
    for peer in peers:
        pl.semaphore_signal(barrier, inc=1, device_id=peer, device_id_type=MESH)
    for h in range(2):
        @pl.when(jnp.logical_not(stays[h]))
        def _():
            pl.semaphore_signal(barrier, inc=1, device_id=across[h], device_id_type=MESH)
    pl.semaphore_wait(barrier, len(peers) + jnp.where(c // 2 == r, 1, 2))

    row_from = c // 2
    for t in range(2):
        for h in range(2):
            src = rot_ref.at[t, pl.ds(2 * h, 2)]
            dst = rc.at[t, :, row_from // Z, row_from % Z, core]
            there = remote(src, dst, tr_s.at[t, h], tr_r.at[t, core], across[h])
            here = pltpu.make_async_copy(src, dst, tr_r.at[t, core])

            @pl.when(stays[h])
            def _():
                here.start()

            @pl.when(jnp.logical_not(stays[h]))
            def _():
                there.start()

        go(remote(
            rot_ref.at[t], rr.at[t, :, y, xh, core], xh_s.at[t], xh_r.at[t], xh_mate
        ))

    def z_block(t, origin, part=None):
        if part is None:
            return rc.at[t, :, :, origin]
        return rc.at[t, :, part, origin]

    def y_block(t, origin, part=None):
        if part is None:
            return rr.at[t, :, origin, :, core]
        return rr.at[t, :, origin, part, core]

    rings = {
        "z": (z_block, z, Z, z_s, z_r, z_next, z_prev),
        "y": (y_block, y, Y, y_s, y_r, y_next, y_prev),
    }

    def ring_send(name, t, s):
        block, me, n, send, recv, nxt, prv = rings[name]
        last = s == n // 2
        for way, (step, device) in enumerate(((-1, nxt), (1, prv))):
            origin = (me + step * (s - 1) + n) % n
            ref = block(t, origin, way if last else None)
            go(remote(ref, ref, send.at[t, way, s - 1], recv.at[t, way, s - 1], device))

    def ring_wait(name, t, s):
        block, me, n, send, recv, nxt, prv = rings[name]
        last = s == n // 2
        for way, (step, device) in enumerate(((-1, nxt), (1, prv))):
            origin = (me + step * s + n) % n
            ref = block(t, origin, way if last else None)
            remote(
                ref, ref, send.at[t, way, s - 1], recv.at[t, way, s - 1], device
            ).wait_recv()

    def mate_copy(t, origin):
        ref = rr.at[t, :, origin, :, core]
        return remote(ref, ref, mt_s.at[t, origin], mt_r.at[t, origin], mate)

    def mate_wait(t):
        for origin in range(Y):
            ref = rr.at[t, :, origin, :, 1 - core]
            remote(ref, ref, mt_s.at[t, origin], mt_r.at[t, origin], mate).wait_recv()

    def ring_begin(t):
        for s in range(2):
            ref = rc.at[t, :, xl, z, s]
            remote(ref, ref, tr_s.at[t, s], tr_r.at[t, s], mate).wait_recv()
        ref = rc.at[t, :, xl, z]
        go(remote(ref, ref, xl_s.at[t], xl_r.at[t], xl_mate))
        own[t].wait()
        ref = rr.at[t, :, y, 1 - xh, core]
        remote(ref, ref, xh_s.at[t], xh_r.at[t], xh_mate).wait_recv()
        ring_send("y", t, 1)
        go(mate_copy(t, y))
        ref = rc.at[t, :, 1 - xl, z]
        remote(ref, ref, xl_s.at[t], xl_r.at[t], xl_mate).wait_recv()
        ring_send("z", t, 1)

    def ring_steps(t):
        for s in range(1, 5):
            ring_wait("z", t, s)
            if s < 4:
                ring_send("z", t, s + 1)
            ring_wait("y", t, s)
            if s < 4:
                ring_send("y", t, s + 1)
                go(mate_copy(t, (y + Y - s) % Y))
            go(mate_copy(t, (y + s) % Y))
        mate_wait(t)

    def split_cols(t):
        for k in range(2):
            high, low = split(rc[t, k].reshape(PAIR, PAIR))
            rcs[t, k, 0] = high
            rcs[t, k, 1] = low

    def split_rows(t):
        def one(k, _):
            high, low = split(rr[t, k].reshape(PAIR, PAIR).T)
            rrt[t, k, 0] = high
            rrt[t, k, 1] = low
            return 0
        lax.fori_loop(0, RP, one, 0)

    def col_flag(t):
        return pair_ref[t, c * CB + 1] - (c * CB + 1)

    def row_flag(t, which):
        first = r * RB + 1 + 4 * which
        return pair_ref[t, first] - first

    def pick(flag, stay, other):
        return jnp.where(jnp.full(stay.shape, flag, jnp.int32) != 0, other, stay)

    ring_begin(0)
    ring_steps(0)
    load.wait()
    ring_begin(1)

    split_cols(0)
    flag = col_flag(0)
    x_copies = {}
    for k in (0, 3, 1, 2):
        rows = pl.ds(k * PAIR, PAIR)
        one = dot3(split(cbuf[rows, :PAIR]), (rcs[0, 0, 0], rcs[0, 0, 1]))
        xs[k, 0] = one[:, :BLOCK]
        two = dot3(split(cbuf[rows, PAIR:]), (rcs[0, 1, 0], rcs[0, 1, 1]))
        xs[k, 1] = two[:, BLOCK:]
        to_left = remote(xs.at[k, 0], xr.at[k, 1], cx_s.at[k, 0], cx_r.at[k, 1], left)
        to_right = remote(xs.at[k, 1], xr.at[k, 0], cx_s.at[k, 1], cx_r.at[k, 0], right)
        x_copies[k] = (to_left, to_right)

        @pl.when(has_left)
        def _():
            to_left.start()

        @pl.when(has_right)
        def _():
            to_right.start()

        b1, b2 = one[:, BLOCK:], two[:, :BLOCK]
        wmid[rows, :BLOCK] = pick(flag, b1, b2)
        wmid[rows, BLOCK:] = pick(flag, b2, b1)

    split_rows(0)
    vx = {}

    def exchange_rows(buf, got, send, recv, half, which, table):
        edge, device, has = ((0, up, has_up), (RB - 1, down, has_down))[which]
        copy = remote(
            buf.at[half, edge], got.at[half, 1 - which],
            send.at[half, which], recv.at[half, 1 - which], device,
        )
        table[half, which] = (copy, has)

        @pl.when(has)
        def _():
            copy.start()

    def await_rows(buf, got, send, recv, half, which):
        edge, device, has = ((0, up, has_up), (RB - 1, down, has_down))[which]
        copy = remote(
            buf.at[half, edge], got.at[half, which],
            send.at[half, which], recv.at[half, which], device,
        )

        @pl.when(has)
        def _():
            copy.wait_recv()

        @pl.when(jnp.logical_not(has))
        def _():
            got[half, which] = buf[half, edge]

    def mix_rows(t, k, value, buf, half):
        out = dot3((rrt[t, k, 0], rrt[t, k, 1]), split(value))
        buf[half, 2 * k] = out[:BLOCK]
        buf[half, 2 * k + 1] = out[BLOCK:]

    for k in (0, 3, 1, 2):
        mix_rows(0, k, wmid[pl.ds(k * PAIR, PAIR), :], v, 0)
        if k == 0:
            exchange_rows(v, vr, vx_s, vx_r, 0, 0, vx)
        if k == 3:
            exchange_rows(v, vr, vx_s, vx_r, 0, 1, vx)

    ring_steps(1)
    split_rows(1)
    split_cols(1)

    flags = [row_flag(0, 0), row_flag(0, 1)]

    def second_rows(half, k):
        if k == 0:
            pair = (vr[half, 0], pick(flags[0], v[half, 1], v[half, 2]))
        elif k == 1:
            pair = (pick(flags[0], v[half, 2], v[half, 1]), v[half, 4])
        elif k == 2:
            pair = (v[half, 3], pick(flags[1], v[half, 5], v[half, 6]))
        else:
            pair = (pick(flags[1], v[half, 6], v[half, 5]), vr[half, 1])
        mix_rows(1, k, jnp.concatenate(pair, axis=0), u, half)

    ux = {}

    def outer_rows(half):
        for which, k in ((0, 0), (1, 3)):
            await_rows(v, vr, vx_s, vx_r, half, which)
            second_rows(half, k)
            exchange_rows(u, ur, ux_s, ux_r, half, which, ux)

    second_rows(0, 1)
    second_rows(0, 2)
    outer_rows(0)

    def await_side(k, side, own_buf, got, send, recv):
        device, has = ((left, has_left), (right, has_right))[side]
        copy = remote(own_buf.at[k, side], got.at[k, side], send.at[k, side], recv.at[k, side], device)

        @pl.when(has)
        def _():
            copy.wait_recv()

        @pl.when(jnp.logical_not(has))
        def _():
            got[k, side] = own_buf[k, side]

    for k in (0, 3, 1, 2):
        for side in range(2):
            await_side(k, side, xs, xr, cx_s, cx_r)
        mix_rows(0, k, jnp.concatenate((xr[k, 0], xr[k, 1]), axis=1), v, 1)
        if k == 0:
            exchange_rows(v, vr, vx_s, vx_r, 1, 0, vx)
        if k == 3:
            exchange_rows(v, vr, vx_s, vx_r, 1, 1, vx)

    second_rows(1, 1)
    second_rows(1, 2)

    t_copies = {}
    flag2 = col_flag(1)

    def second_cols(g, refs):
        mid = jnp.concatenate([buf[0, i] for buf, i in refs], axis=0)
        edge = jnp.concatenate([buf[1, i] for buf, i in refs], axis=0)
        one = dot3(
            split(jnp.concatenate((edge[:, :BLOCK], mid[:, :BLOCK]), axis=1)),
            (rcs[1, 0, 0], rcs[1, 0, 1]),
        )
        ts[g, 0] = one[:, :BLOCK]
        two = dot3(
            split(jnp.concatenate((mid[:, BLOCK:], edge[:, BLOCK:]), axis=1)),
            (rcs[1, 1, 0], rcs[1, 1, 1]),
        )
        ts[g, 1] = two[:, BLOCK:]
        to_left = remote(ts.at[g, 0], tr.at[g, 1], tx_s.at[g, 0], tx_r.at[g, 1], left)
        to_right = remote(ts.at[g, 1], tr.at[g, 0], tx_s.at[g, 1], tx_r.at[g, 0], right)
        t_copies[g] = (to_left, to_right)

        @pl.when(has_left)
        def _():
            to_left.start()

        @pl.when(has_right)
        def _():
            to_right.start()

        b1, b2 = one[:, BLOCK:], two[:, :BLOCK]
        tmid[g, :, :BLOCK] = pick(flag2, b1, b2)
        tmid[g, :, BLOCK:] = pick(flag2, b2, b1)

    second_cols(0, ((u, 2), (u, 3)))
    second_cols(1, ((u, 4), (u, 5)))
    outer_rows(1)
    second_cols(2, ((u, 1), (u, 6)))
    for half in range(2):
        for which in range(2):
            await_rows(u, ur, ux_s, ux_r, half, which)
    second_cols(3, ((ur, 0), (ur, 1)))

    places = {1: (2, 0), 2: (0, 0), 3: (0, 1), 4: (1, 0), 5: (1, 1), 6: (2, 1), 0: (3, 0), 7: (3, 1)}
    finals = [row_flag(1, 0), row_flag(1, 1)]

    def parts(block):
        g, half = places[block]
        rows = pl.ds(half * BLOCK, BLOCK)
        return tr[g, 0, rows], tmid[g, rows], tr[g, 1, rows]

    outs = []

    def emit(position, flag, stay, other=None):
        rows = pl.ds(position * BLOCK, BLOCK)
        values = parts(stay)
        if other is not None:
            values = [pick(flag, a, b) for a, b in zip(values, parts(other))]
        obuf[rows, :BLOCK] = values[0]
        obuf[rows, BLOCK:3 * BLOCK] = values[1]
        obuf[rows, 3 * BLOCK:] = values[2]
        copy = pltpu.make_async_copy(obuf.at[rows], out_ref.at[rows], out_sem.at[position])
        copy.start()
        outs.append(copy)

    def await_group(g):
        for side in range(2):
            await_side(g, side, ts, tr, tx_s, tx_r)

    await_group(0)
    emit(4, None, 3)
    await_group(1)
    emit(3, None, 4)
    await_group(2)
    emit(1, finals[0], 1, 2)
    emit(2, finals[0], 2, 1)
    emit(5, finals[1], 5, 6)
    emit(6, finals[1], 6, 5)
    await_group(3)
    emit(0, None, 0)
    emit(7, None, 7)

    for copy in started:
        copy.wait_send()
    for t in range(2):
        for h in range(2):
            src = rot_ref.at[t, pl.ds(2 * h, 2)]
            dst = rc.at[t, :, row_from // Z, row_from % Z, core]
            there = remote(src, dst, tr_s.at[t, h], tr_r.at[t, core], across[h])

            @pl.when(jnp.logical_not(stays[h]))
            def _():
                there.wait_send()

    for table in (x_copies, t_copies):
        for to_left, to_right in table.values():
            @pl.when(has_left)
            def _():
                to_left.wait_send()

            @pl.when(has_right)
            def _():
                to_right.wait_send()

    for table in (vx, ux):
        for copy, has in table.values():
            @pl.when(has)
            def _():
                copy.wait_send()

    for copy in outs:
        copy.wait()


def body(covariance, rotations, pairing):
    dma = pltpu.SemaphoreType.DMA
    tile = covariance.shape
    scratch = [
        pltpu.VMEM(tile, F32),
        pltpu.VMEM((2, RP, Y, XH, CORE, 8, PAIR), F32),
        pltpu.VMEM((2, 2, XL, Z, 2, 8, PAIR), F32),
        pltpu.VMEM((2, RP, 2, PAIR, PAIR), B16),
        pltpu.VMEM((2, 2, 2, PAIR, PAIR), B16),
        pltpu.VMEM((4, 2, PAIR, BLOCK), F32),
        pltpu.VMEM((4, 2, PAIR, BLOCK), F32),
        pltpu.VMEM((tile[0], PAIR), F32),
        pltpu.VMEM((2, RB, BLOCK, PAIR), F32),
        pltpu.VMEM((2, 2, BLOCK, PAIR), F32),
        pltpu.VMEM((2, RB, BLOCK, PAIR), F32),
        pltpu.VMEM((2, 2, BLOCK, PAIR), F32),
        pltpu.VMEM((4, 2, PAIR, BLOCK), F32),
        pltpu.VMEM((4, 2, PAIR, BLOCK), F32),
        pltpu.VMEM((4, PAIR, PAIR), F32),
        pltpu.VMEM(tile, F32),
        dma((3,)),
        dma((2, 2)), dma((2, 2)),
        dma((2,)), dma((2,)),
        dma((2,)), dma((2,)),
        dma((2, 2, 4)), dma((2, 2, 4)),
        dma((2, 2, 4)), dma((2, 2, 4)),
        dma((2, Y)), dma((2, Y)),
        dma((4, 2)), dma((4, 2)),
        dma((2, 2)), dma((2, 2)),
        dma((2, 2)), dma((2, 2)),
        dma((4, 2)), dma((4, 2)),
        dma((RB,)),
    ]
    return pl.pallas_call(
        kernel,
        out_shape=jax.ShapeDtypeStruct(tile, F32),
        in_specs=[
            pl.BlockSpec(memory_space=pl.ANY),
            pl.BlockSpec(memory_space=pl.ANY),
            pl.BlockSpec(memory_space=pltpu.SMEM),
        ],
        out_specs=pl.BlockSpec(memory_space=pl.ANY),
        scratch_shapes=scratch,
        compiler_params=pltpu.CompilerParams(
            collective_id=0, has_side_effects=True, vmem_limit_bytes=48 * 2**20
        ),
        cost_estimate=pl.CostEstimate(
            flops=2 * 4 * tile[0] * tile[1] * PAIR, bytes_accessed=8 * tile[0] * tile[1],
            transcendentals=0,
        ),
    )(covariance, rotations, pairing)


def solution(mesh):
    in_specs = (P("row", "col"), P(None, "row", "col", None), P())
    out_specs = P("row", "col")
    return jax.shard_map(body, mesh=mesh, in_specs=in_specs, out_specs=out_specs, check_vma=False)
```

```python
import jax
import jax.numpy as jnp
from jax import lax
from jax.experimental import pallas as pl
from jax.experimental.pallas import tpu as pltpu
from jax.sharding import PartitionSpec as P

BLOCK = 128
PAIR = 2 * BLOCK
ROWS, COLS = 16, 32
XL, Z, Y, XH, CORE = 2, 8, 8, 2, 2
RB, CB = 8, 4
RP = RB // 2
MESH = pl.DeviceIdType.MESH
F32, B16 = jnp.float32, jnp.bfloat16


def split(value):
    high = value.astype(B16)
    low = (value - high.astype(F32)).astype(B16)
    return high, low


def dot(a, b):
    return jnp.dot(a, b, preferred_element_type=F32)


def dot3(a, b):
    return dot(a[0], b[0]) + (dot(a[0], b[1]) + dot(a[1], b[0]))


def kernel(
    cov_ref, rot_ref, pair_ref, out_ref,
    cbuf, rr, rc, rrt, rcs, v, vr, u, ur, xs, xr, xmid, ts, tr, tmid, obuf,
    loc_sem, tr_s, tr_r, xl_s, xl_r, xh_s, xh_r, z_s, z_r, y_s, y_r, mt_s, mt_r,
    vx_s, vx_r, ux_s, ux_r, cx_s, cx_r, tx_s, tx_r, out_sem,
):
    r = lax.axis_index("row")
    c = lax.axis_index("col")
    xl, z = r // Z, r % Z
    y, xh, core = c // 4, (c // 2) % 2, c % 2

    def z_dev(step):
        return (xl * Z + (z + step + Z) % Z, c)

    def y_dev(step):
        return (r, ((y + step + Y) % Y) * 4 + xh * 2 + core)

    mate = (r, y * 4 + xh * 2 + (1 - core))
    xh_mate = (r, y * 4 + (1 - xh) * 2 + core)
    xl_mate = ((1 - xl) * Z + z, c)
    up = ((r + ROWS - 1) % ROWS, c)
    down = ((r + 1) % ROWS, c)
    left = (r, (c + COLS - 1) % COLS)
    right = (r, (c + 1) % COLS)
    across = [(c // 2, 2 * r + h) for h in range(2)]
    diagonal = c // 2 == r
    stays = [jnp.logical_and(diagonal, core == h) for h in range(2)]
    ends = ((0, up, r > 0), (RB - 1, down, r < ROWS - 1))
    sides = ((left, c > 0), (right, c < COLS - 1))

    def remote(src, dst, send, recv, device):
        return pltpu.make_async_remote_copy(
            src_ref=src, dst_ref=dst, send_sem=send, recv_sem=recv,
            device_id=device, device_id_type=MESH,
        )

    started = []

    def go(copy):
        copy.start()
        started.append(copy)

    def arrived(ref, recv):
        remote(ref, ref, loc_sem.at[0], recv, mate).wait_recv()

    load = pltpu.make_async_copy(cov_ref, cbuf, loc_sem.at[0])
    load.start()
    own = [
        pltpu.make_async_copy(rot_ref.at[t], rr.at[t, :, y, xh, core], loc_sem.at[1 + t])
        for t in range(2)
    ]
    for t in range(2):
        own[t].start()

    barrier = pltpu.get_barrier_semaphore()
    peers = [mate, xh_mate, xl_mate, up, down, left, right]
    peers += [dev(step) for dev in (z_dev, y_dev) for step in (1, -1, 2, -2)]
    for peer in peers:
        pl.semaphore_signal(barrier, inc=1, device_id=peer, device_id_type=MESH)
    for h in range(2):
        @pl.when(jnp.logical_not(stays[h]))
        def _():
            pl.semaphore_signal(barrier, inc=1, device_id=across[h], device_id_type=MESH)
    pl.semaphore_wait(barrier, len(peers) + jnp.where(diagonal, 1, 2))

    def across_copy(t, h):
        src = rot_ref.at[t, pl.ds(2 * h, 2)]
        dst = rc.at[t, :, c // 2 // Z, c // 2 % Z, core]
        there = remote(src, dst, tr_s.at[t, h], tr_r.at[t, core], across[h])
        here = pltpu.make_async_copy(src, dst, tr_r.at[t, core])
        return there, here

    def across_send(t):
        for h in range(2):
            there, here = across_copy(t, h)

            @pl.when(stays[h])
            def _():
                here.start()

            @pl.when(jnp.logical_not(stays[h]))
            def _():
                there.start()

    def y_block(t, origin, half=None):
        if half is None:
            return rr.at[t, :, origin, xh, core]
        return rr.at[t, pl.ds(2 * half, 2), origin, xh, core]

    def z_block(t, origin, half=None):
        if half is None:
            return rc.at[t, :, :, origin]
        return rc.at[t, :, half, origin]

    STEPS = (1, -1, 2, -2, 3, -3)

    def spread_rows(t, origin, src=None):
        ref = y_block(t, origin)
        src = ref if src is None else src
        go(remote(src, ref, xh_s.at[t, origin], xh_r.at[t, origin], xh_mate))
        go(remote(src, ref, mt_s.at[t, origin, 0], mt_r.at[t, origin, xh], mate))

    def first_level(block, t, me, send, recv, dev, src=None):
        ref = block(t, me)
        src = ref if src is None else src
        for i in range(4):
            go(remote(src, ref, send.at[t, i], recv.at[t, i], dev(STEPS[i])))

    def second_level(block, t, me, n, send, recv, dev, then=None):
        for i in (2, 3):
            way = 1 if i == 2 else -1
            origin = (me - 2 * way + n) % n
            ref = block(t, origin)
            arrived(ref, recv.at[t, i])
            go(remote(ref, ref, send.at[t, i + 2], recv.at[t, i + 2], dev(way)))
            part = block(t, origin, i - 2)
            go(remote(part, part, send.at[t, i + 4], recv.at[t, i + 4], dev(2 * way)))
            if then is not None:
                then(t, origin)
        for i in (0, 1):
            origin = (me - STEPS[i] + n) % n
            arrived(block(t, origin), recv.at[t, i])
            if then is not None:
                then(t, origin)

    def third_level(block, t, me, n, recv, then=None):
        for i in (4, 5):
            origin = (me - STEPS[i] + n) % n
            arrived(block(t, origin), recv.at[t, i])
            if then is not None:
                then(t, origin)
        origin = (me + n // 2) % n
        for half in range(2):
            arrived(block(t, origin, half), recv.at[t, 6 + half])
        if then is not None:
            then(t, origin)

    def y_first(t):
        piece = rot_ref.at[t]
        first_level(y_block, t, y, y_s, y_r, y_dev, piece)
        spread_rows(t, y, piece)

    def y_second(t):
        second_level(y_block, t, y, Y, y_s, y_r, y_dev, spread_rows)

    def y_third(t):
        third_level(y_block, t, y, Y, y_r, spread_rows)

    def x_pass(t):
        for step in (0, 1, -1, 2, -2, 3, -3, 4):
            origin = (y + step + Y) % Y
            ref = rr.at[t, :, origin, 1 - xh, core]
            arrived(ref, xh_r.at[t, origin])
            go(remote(ref, ref, mt_s.at[t, origin, 1], mt_r.at[t, origin, 1 - xh], mate))

    def mate_wait(t):
        for origin in range(Y):
            for side in range(2):
                arrived(rr.at[t, :, origin, side, 1 - core], mt_r.at[t, origin, side])
        own[t].wait()

    def z_begin(t):
        for s in range(2):
            arrived(rc.at[t, :, xl, z, s], tr_r.at[t, s])
        ref = rc.at[t, :, xl, z]
        go(remote(ref, ref, xl_s.at[t], xl_r.at[t], xl_mate))

    def z_first(t):
        arrived(rc.at[t, :, 1 - xl, z], xl_r.at[t])
        first_level(z_block, t, z, z_s, z_r, z_dev)

    def z_second(t):
        second_level(z_block, t, z, Z, z_s, z_r, z_dev)

    def z_third(t):
        third_level(z_block, t, z, Z, z_r)

    def split_cols(t):
        for k in range(2):
            high, low = split(rc[t, k].reshape(PAIR, PAIR))
            rcs[t, k, 0] = high
            rcs[t, k, 1] = low

    def split_rows(t):
        def one(k, _):
            high, low = split(rr[t, k].reshape(PAIR, PAIR).T)
            rrt[t, k, 0] = high
            rrt[t, k, 1] = low
            return 0
        lax.fori_loop(0, RP, one, 0)

    def col_flag(t):
        return pair_ref[t, c * CB + 1] - (c * CB + 1)

    def row_flag(t, which):
        first = r * RB + 1 + 4 * which
        return pair_ref[t, first] - first

    def pick(flag, stay, other):
        return jnp.where(jnp.full(stay.shape, flag, jnp.int32) != 0, other, stay)

    def mix_rows(t, k, value, buf):
        out = dot3((rrt[t, k, 0], rrt[t, k, 1]), split(value))
        buf[2 * k] = out[:BLOCK]
        buf[2 * k + 1] = out[BLOCK:]

    row_copies = []

    def send_row(buf, got, send, recv, which):
        edge, device, has = ends[which]
        copy = remote(buf.at[edge], got.at[1 - which], send.at[which], recv.at[1 - which], device)
        row_copies.append((copy, has))

        @pl.when(has)
        def _():
            copy.start()

    def await_row(buf, got, recv, which):
        edge, device, has = ends[which]

        @pl.when(has)
        def _():
            arrived(got.at[which], recv.at[which])

        @pl.when(jnp.logical_not(has))
        def _():
            got[which] = buf[edge]

    flags = [row_flag(0, 0), row_flag(0, 1)]

    def second_rows(k):
        if k == 0:
            pair = (vr[0], pick(flags[0], v[1], v[2]))
        elif k == 1:
            pair = (pick(flags[0], v[2], v[1]), v[4])
        elif k == 2:
            pair = (v[3], pick(flags[1], v[5], v[6]))
        else:
            pair = (pick(flags[1], v[6], v[5]), vr[1])
        mix_rows(1, k, jnp.concatenate(pair, axis=0), u)

    groups = (((u, 2), (u, 3)), ((u, 4), (u, 5)), ((u, 1), (u, 6)), ((ur, 0), (ur, 1)))
    side_copies = []

    def mix_cols(t, g, first, second, outer, middle, got, send, recv):
        one = dot3(split(first), (rcs[t, 0, 0], rcs[t, 0, 1]))
        outer[g, 0] = one[:, :BLOCK]
        two = dot3(split(second), (rcs[t, 1, 0], rcs[t, 1, 1]))
        outer[g, 1] = two[:, BLOCK:]
        for side, (device, has) in enumerate(sides):
            copy = remote(
                outer.at[g, side], got.at[g, 1 - side],
                send.at[g, side], recv.at[g, 1 - side], device,
            )
            side_copies.append((copy, has))

            @pl.when(has)
            def _():
                copy.start()

        flag = col_flag(t)
        b1, b2 = one[:, BLOCK:], two[:, :BLOCK]
        middle[g, :, :BLOCK] = pick(flag, b1, b2)
        middle[g, :, BLOCK:] = pick(flag, b2, b1)

    def await_sides(g, outer, got, recv):
        for side, (device, has) in enumerate(sides):
            @pl.when(has)
            def _():
                arrived(got.at[g, side], recv.at[g, side])

            @pl.when(jnp.logical_not(has))
            def _():
                got[g, side] = outer[g, side]

    def first_cols(g):
        rows = jnp.concatenate([buf[i] for buf, i in groups[g]], axis=0)
        mix_cols(0, g, rows[:, :PAIR], rows[:, PAIR:], xs, xmid, xr, cx_s, cx_r)

    def second_cols(g):
        await_sides(g, xs, xr, cx_r)
        first = jnp.concatenate((xr[g, 0], xmid[g, :, :BLOCK]), axis=1)
        second = jnp.concatenate((xmid[g, :, BLOCK:], xr[g, 1]), axis=1)
        mix_cols(1, g, first, second, ts, tmid, tr, tx_s, tx_r)

    across_send(0)
    y_first(0)
    across_send(1)
    y_first(1)
    y_second(0)
    y_second(1)
    z_begin(0)
    z_first(0)
    y_third(0)
    z_begin(1)
    y_third(1)
    x_pass(0)
    z_second(0)
    z_first(1)
    mate_wait(0)
    load.wait()

    split_rows(0)
    for k in (0, 3, 1, 2):
        mix_rows(0, k, cbuf[pl.ds(k * PAIR, PAIR), :], v)
        if k in (0, 3):
            send_row(v, vr, vx_s, vx_r, k // 3)
    x_pass(1)
    z_third(0)
    split_cols(0)
    z_second(1)
    mate_wait(1)
    split_rows(1)
    second_rows(1)
    first_cols(0)
    second_rows(2)
    first_cols(1)
    for which, k in ((0, 0), (1, 3)):
        await_row(v, vr, vx_r, which)
        second_rows(k)
        send_row(u, ur, ux_s, ux_r, which)
    first_cols(2)
    z_third(1)
    split_cols(1)
    second_cols(0)
    second_cols(1)
    for which in range(2):
        await_row(u, ur, ux_r, which)
    first_cols(3)
    second_cols(2)
    second_cols(3)

    places = {1: (2, 0), 2: (0, 0), 3: (0, 1), 4: (1, 0), 5: (1, 1), 6: (2, 1), 0: (3, 0), 7: (3, 1)}
    finals = [row_flag(1, 0), row_flag(1, 1)]

    def parts(block):
        g, half = places[block]
        rows = pl.ds(half * BLOCK, BLOCK)
        return tr[g, 0, rows], tmid[g, rows], tr[g, 1, rows]

    outs = []

    def emit(position, flag, stay, other=None):
        rows = pl.ds(position * BLOCK, BLOCK)
        values = parts(stay)
        if other is not None:
            values = [pick(flag, a, b) for a, b in zip(values, parts(other))]
        obuf[rows, :BLOCK] = values[0]
        obuf[rows, BLOCK:3 * BLOCK] = values[1]
        obuf[rows, 3 * BLOCK:] = values[2]
        copy = pltpu.make_async_copy(obuf.at[rows], out_ref.at[rows], out_sem.at[position])
        copy.start()
        outs.append(copy)

    await_sides(0, ts, tr, tx_r)
    emit(4, None, 3)
    await_sides(1, ts, tr, tx_r)
    emit(3, None, 4)
    await_sides(2, ts, tr, tx_r)
    emit(1, finals[0], 1, 2)
    emit(2, finals[0], 2, 1)
    emit(5, finals[1], 5, 6)
    emit(6, finals[1], 6, 5)
    await_sides(3, ts, tr, tx_r)
    emit(0, None, 0)
    emit(7, None, 7)

    for copy in started:
        copy.wait_send()
    for t in range(2):
        for h in range(2):
            there, here = across_copy(t, h)

            @pl.when(jnp.logical_not(stays[h]))
            def _():
                there.wait_send()

    for copy, has in row_copies + side_copies:
        @pl.when(has)
        def _():
            copy.wait_send()

    for copy in outs:
        copy.wait()


def body(covariance, rotations, pairing):
    dma = pltpu.SemaphoreType.DMA
    tile = covariance.shape
    wide = (BLOCK, tile[1])
    outer = pltpu.VMEM((4, 2, PAIR, BLOCK), F32)
    middle = pltpu.VMEM((4, PAIR, PAIR), F32)
    scratch = [
        pltpu.VMEM(tile, F32),
        pltpu.VMEM((2, RP, Y, XH, CORE, 8, PAIR), F32),
        pltpu.VMEM((2, 2, XL, Z, 2, 8, PAIR), F32),
        pltpu.VMEM((2, RP, 2, PAIR, PAIR), B16),
        pltpu.VMEM((2, 2, 2, PAIR, PAIR), B16),
        pltpu.VMEM((RB, *wide), F32),
        pltpu.VMEM((2, *wide), F32),
        pltpu.VMEM((RB, *wide), F32),
        pltpu.VMEM((2, *wide), F32),
        outer, outer, middle,
        outer, outer, middle,
        pltpu.VMEM(tile, F32),
        dma((3,)),
        dma((2, 2)), dma((2, 2)),
        dma((2,)), dma((2,)),
        dma((2, Y)), dma((2, Y)),
        dma((2, 8)), dma((2, 8)),
        dma((2, 8)), dma((2, 8)),
        dma((2, Y, 2)), dma((2, Y, 2)),
        dma((2,)), dma((2,)),
        dma((2,)), dma((2,)),
        dma((4, 2)), dma((4, 2)),
        dma((4, 2)), dma((4, 2)),
        dma((RB,)),
    ]
    return pl.pallas_call(
        kernel,
        out_shape=jax.ShapeDtypeStruct(tile, F32),
        in_specs=[
            pl.BlockSpec(memory_space=pltpu.HBM),
            pl.BlockSpec(memory_space=pltpu.HBM),
            pl.BlockSpec(memory_space=pltpu.SMEM),
        ],
        out_specs=pl.BlockSpec(memory_space=pl.ANY),
        scratch_shapes=scratch,
        compiler_params=pltpu.CompilerParams(
            collective_id=0, has_side_effects=True, vmem_limit_bytes=60 * 2**20
        ),
        cost_estimate=pl.CostEstimate(
            flops=2 * 4 * tile[0] * tile[1] * PAIR, bytes_accessed=8 * tile[0] * tile[1],
            transcendentals=0,
        ),
    )(covariance, rotations, pairing)


def solution(mesh):
    in_specs = (P("row", "col"), P(None, "row", "col", None), P())
    out_specs = P("row", "col")
    return jax.shard_map(body, mesh=mesh, in_specs=in_specs, out_specs=out_specs, check_vma=False)
```

```python
import jax
import jax.numpy as jnp
from jax import lax
from jax.experimental import pallas as pl
from jax.experimental.pallas import tpu as pltpu
from jax.sharding import PartitionSpec as P

BLOCK = 128
PAIR = 2 * BLOCK
ROWS, COLS = 16, 32
XL, Z, Y, XH, CORE = 2, 8, 8, 2, 2
RB, CB = 8, 4
RP = RB // 2
MESH = pl.DeviceIdType.MESH
F32, B16 = jnp.float32, jnp.bfloat16


def split(value):
    high = value.astype(B16)
    low = (value - high.astype(F32)).astype(B16)
    return high, low


def dot(a, b):
    return jnp.dot(a, b, preferred_element_type=F32)


def dot3(a, b):
    return dot(a[0], b[0]) + (dot(a[0], b[1]) + dot(a[1], b[0]))


def kernel(
    cov_ref, rot_ref, pair_ref, out_ref,
    cbuf, halo, rr, rc0, rc, rrt, qs, rcs, w, v, vr, u, ur, ts, tr, tmid, obuf,
    loc_sem, h_s, h_r, t0_s, t0_r, tr_s, tr_r, xl_s, xl_r, xh_s, xh_r, z_s, z_r, y_s, y_r, mt_s, mt_r,
    vx_s, vx_r, ux_s, ux_r, tx_s, tx_r, out_sem,
):
    r = lax.axis_index("row")
    c = lax.axis_index("col")
    xl, z = r // Z, r % Z
    y, xh, core = c // 4, (c // 2) % 2, c % 2

    def z_dev(step):
        return (xl * Z + (z + step + Z) % Z, c)

    def y_dev(step):
        return (r, ((y + step + Y) % Y) * 4 + xh * 2 + core)

    mate = (r, y * 4 + xh * 2 + (1 - core))
    xh_mate = (r, y * 4 + (1 - xh) * 2 + core)
    xl_mate = ((1 - xl) * Z + z, c)
    up = ((r + ROWS - 1) % ROWS, c)
    down = ((r + 1) % ROWS, c)
    left = (r, (c + COLS - 1) % COLS)
    right = (r, (c + 1) % COLS)
    across = [(c // 2, 2 * r + h) for h in range(2)]
    diagonal = c // 2 == r
    stays = [jnp.logical_and(diagonal, core == h) for h in range(2)]
    ends = ((0, up, r > 0), (RB - 1, down, r < ROWS - 1))
    sides = ((left, c > 0), (right, c < COLS - 1))

    def remote(src, dst, send, recv, device):
        return pltpu.make_async_remote_copy(
            src_ref=src, dst_ref=dst, send_sem=send, recv_sem=recv,
            device_id=device, device_id_type=MESH,
        )

    started = []

    def go(copy):
        copy.start()
        started.append(copy)

    def arrived(ref, recv):
        remote(ref, ref, loc_sem.at[0], recv, mate).wait_recv()

    load = pltpu.make_async_copy(cov_ref, cbuf, loc_sem.at[0])
    load.start()
    own = [
        pltpu.make_async_copy(rot_ref.at[t], rr.at[t, :, y, xh, core], loc_sem.at[1 + t])
        for t in range(2)
    ]
    for t in range(2):
        own[t].start()

    barrier = pltpu.get_barrier_semaphore()
    peers = [mate, xh_mate, xl_mate, up, down, left, right]
    peers += [dev(step) for dev in (z_dev, y_dev) for step in (1, -1, 2, -2)]
    for peer in peers:
        pl.semaphore_signal(barrier, inc=1, device_id=peer, device_id_type=MESH)
    beside = c // 2 + jnp.where(core == 0, -1, 1)
    has_beside = jnp.logical_and(beside >= 0, beside < ROWS)
    for s in range(2):
        @pl.when(jnp.logical_not(jnp.logical_and(diagonal, core == s)))
        def _():
            pl.semaphore_signal(barrier, inc=1, device_id=(c // 2, 2 * r + s), device_id_type=MESH)

        @pl.when(has_beside)
        def _():
            pl.semaphore_signal(
                barrier, inc=1, device_id=((beside + ROWS) % ROWS, 2 * r + s), device_id_type=MESH
            )
    targets = 2 + jnp.where(r > 0, 1, 0) + jnp.where(r < ROWS - 1, 1, 0) - jnp.where(diagonal, 1, 0)
    pl.semaphore_wait(barrier, len(peers) + targets)

    def halo_send(k):
        rows = pl.ds(k * PAIR, PAIR)
        for side, (device, has) in enumerate(sides):
            src = cov_ref.at[rows, pl.ds(side * PAIR, PAIR)]
            copy = remote(src, halo.at[1 - side, rows], h_s.at[k, side], h_r.at[k, 1 - side], device)
            here = pltpu.make_async_copy(src, halo.at[side, rows], h_r.at[k, side])
            side_copies.append((copy, has))

            @pl.when(has)
            def _():
                copy.start()

            @pl.when(jnp.logical_not(has))
            def _():
                here.start()

    def halo_wait(k):
        for side in range(2):
            arrived(halo.at[side, pl.ds(k * PAIR, PAIR)], h_r.at[k, side])

    side_copies = []

    first_tile = jnp.where(r > 0, 2 * r - 1, 0)
    last_tile = jnp.where(r < ROWS - 1, 2 * r + 2, COLS - 1)
    pieces = (
        (0, 0, first_tile, jnp.where(r > 0, 3, 0)),
        (0, 1, 2 * r, 1), (1, 0, 2 * r, 2), (2, 0, 2 * r, 3),
        (1, 1, 2 * r + 1, 0), (2, 1, 2 * r + 1, 1), (3, 0, 2 * r + 1, 2),
        (3, 1, last_tile, jnp.where(r < ROWS - 1, 0, 3)),
    )
    piece_copies = []

    def pieces_send():
        for i, (k, half, tile, position) in enumerate(pieces):
            src = rot_ref.at[0, k, :, pl.ds(half * BLOCK, BLOCK)]
            dst = rc0.at[position, c // 2 // Z, c // 2 % Z, core]
            there = remote(src, dst, t0_s.at[i], t0_r.at[position, core], (c // 2, tile))
            here = pltpu.make_async_copy(src, dst, t0_r.at[position, core])
            away = jnp.logical_not(jnp.logical_and(diagonal, tile == c))
            piece_copies.append((there, away))

            @pl.when(away)
            def _():
                there.start()

            @pl.when(jnp.logical_not(away))
            def _():
                here.start()

    def across_copy(h):
        src = rot_ref.at[1, pl.ds(2 * h, 2)]
        dst = rc.at[:, c // 2 // Z, c // 2 % Z, core]
        there = remote(src, dst, tr_s.at[h], tr_r.at[core], across[h])
        here = pltpu.make_async_copy(src, dst, tr_r.at[core])
        return there, here

    def across_send():
        for h in range(2):
            there, here = across_copy(h)

            @pl.when(stays[h])
            def _():
                here.start()

            @pl.when(jnp.logical_not(stays[h]))
            def _():
                there.start()

    def y_block(t, origin, half=None):
        if half is None:
            return rr.at[t, :, origin, :, core]
        return rr.at[t, :, origin, half, core]

    def z_block(t, origin, half=None):
        if t == 0:
            return rc0.at[:, :, origin] if half is None else rc0.at[:, half, origin]
        return rc.at[:, :, origin] if half is None else rc.at[:, half, origin]

    STEPS = (1, -1, 2, -2, 3, -3)

    def first_level(block, t, me, send, recv, dev, src=None):
        ref = block(t, me)
        src = ref if src is None else src
        for i in (2, 3, 0, 1):
            go(remote(src, ref, send.at[t, i], recv.at[t, i], dev(STEPS[i])))

    def second_level(block, t, me, n, send, recv, dev, then=None):
        for i in (2, 3):
            way = 1 if i == 2 else -1
            origin = (me - 2 * way + n) % n
            ref = block(t, origin)
            arrived(ref, recv.at[t, i])
            part = block(t, origin, i - 2)
            go(remote(part, part, send.at[t, i + 4], recv.at[t, i + 4], dev(2 * way)))
            go(remote(ref, ref, send.at[t, i + 2], recv.at[t, i + 2], dev(way)))
            if then is not None:
                then(t, origin)
        for i in (0, 1):
            origin = (me - STEPS[i] + n) % n
            arrived(block(t, origin), recv.at[t, i])
            if then is not None:
                then(t, origin)

    def third_level(block, t, me, n, recv, then=None):
        for i in (4, 5):
            origin = (me - STEPS[i] + n) % n
            arrived(block(t, origin), recv.at[t, i])
            if then is not None:
                then(t, origin)
        origin = (me + n // 2) % n
        for half in range(2):
            arrived(block(t, origin, half), recv.at[t, 6 + half])
        if then is not None:
            then(t, origin)

    def y_begin(t):
        go(remote(rot_ref.at[t], rr.at[t, :, y, xh, core], xh_s.at[t], xh_r.at[t], xh_mate))

    def y_first(t):
        own[t].wait()
        arrived(rr.at[t, :, y, 1 - xh, core], xh_r.at[t])
        first_level(y_block, t, y, y_s, y_r, y_dev)

    def y_second(t):
        second_level(y_block, t, y, Y, y_s, y_r, y_dev)

    def y_third(t):
        third_level(y_block, t, y, Y, y_r)
        ref = rr.at[t, :, :, :, core]
        go(remote(ref, ref, mt_s.at[t], mt_r.at[t], mate))

    def mate_wait(t):
        arrived(rr.at[t, :, :, :, 1 - core], mt_r.at[t])

    def z_begin(t):
        for s in range(2):
            if t == 0:
                for position in range(CB):
                    arrived(rc0.at[position, xl, z, s], t0_r.at[position, s])
            else:
                arrived(rc.at[:, xl, z, s], tr_r.at[s])
        ref = rc0.at[:, xl, z] if t == 0 else rc.at[:, xl, z]
        go(remote(ref, ref, xl_s.at[t], xl_r.at[t], xl_mate))

    def z_first(t):
        buf = rc0 if t == 0 else rc
        arrived(buf.at[:, 1 - xl, z], xl_r.at[t])
        first_level(z_block, t, z, z_s, z_r, z_dev)

    def z_second(t):
        second_level(z_block, t, z, Z, z_s, z_r, z_dev)

    def z_third(t):
        third_level(z_block, t, z, Z, z_r)

    def split_first():
        for position in range(CB):
            high, low = split(rc0[position].reshape(PAIR, BLOCK))
            qs[position, 0] = high
            qs[position, 1] = low

    def split_second():
        for k in range(2):
            high, low = split(rc[k].reshape(PAIR, PAIR))
            rcs[k, 0] = high
            rcs[k, 1] = low

    def split_rows(t):
        def one(k, _):
            high, low = split(rr[t, k].reshape(PAIR, PAIR).T)
            rrt[t, k, 0] = high
            rrt[t, k, 1] = low
            return 0
        lax.fori_loop(0, RP, one, 0)

    def col_flag(t):
        return pair_ref[t, c * CB + 1] - (c * CB + 1)

    def row_flag(t, which):
        first = r * RB + 1 + 4 * which
        return pair_ref[t, first] - first

    def pick(flag, stay, other):
        return jnp.where(jnp.full(stay.shape, flag, jnp.int32) != 0, other, stay)

    def mix_rows(t, k, value, buf, cols=slice(None)):
        out = dot3((rrt[t, k, 0], rrt[t, k, 1]), split(value))
        buf[2 * k, :, cols] = out[:BLOCK]
        buf[2 * k + 1, :, cols] = out[BLOCK:]

    row_copies = []
    HALVES = [pl.ds(half * PAIR, PAIR) for half in range(2)]

    def send_row(buf, got, send, recv, which, half):
        edge, device, has = ends[which]
        copy = remote(
            buf.at[edge, :, HALVES[half]], got.at[1 - which, :, HALVES[half]],
            send.at[half, which], recv.at[half, 1 - which], device,
        )
        row_copies.append((copy, has))

        @pl.when(has)
        def _():
            copy.start()

    def await_row(buf, got, recv, which, half):
        edge, device, has = ends[which]
        cols = HALVES[half]

        @pl.when(has)
        def _():
            arrived(got.at[which, :, cols], recv.at[half, which])

        @pl.when(jnp.logical_not(has))
        def _():
            got[which, :, cols] = buf[edge, :, cols]

    flags = [row_flag(0, 0), row_flag(0, 1)]

    def second_rows(k, cols=slice(None)):
        if k == 0:
            pair = (vr[0, :, cols], pick(flags[0], v[1, :, cols], v[2, :, cols]))
        elif k == 1:
            pair = (pick(flags[0], v[2, :, cols], v[1, :, cols]), v[4, :, cols])
        elif k == 2:
            pair = (v[3, :, cols], pick(flags[1], v[5, :, cols], v[6, :, cols]))
        else:
            pair = (pick(flags[1], v[6, :, cols], v[5, :, cols]), vr[1, :, cols])
        mix_rows(1, k, jnp.concatenate(pair, axis=0), u, cols)

    def first_cols(k):
        rows = pl.ds(k * PAIR, PAIR)
        halo_wait(k)
        values = (halo[0, rows], cbuf[rows, :PAIR], cbuf[rows, PAIR:], halo[1, rows])
        out = [dot3(split(value), (qs[p, 0], qs[p, 1])) for p, value in enumerate(values)]
        flag = col_flag(0)
        w[rows, :BLOCK] = out[0]
        w[rows, BLOCK:2 * BLOCK] = pick(flag, out[1], out[2])
        w[rows, 2 * BLOCK:3 * BLOCK] = pick(flag, out[2], out[1])
        w[rows, 3 * BLOCK:] = out[3]

    groups = (((u, 2), (u, 3)), ((u, 4), (u, 5)), ((u, 1), (u, 6)), ((ur, 0), (ur, 1)))

    def second_cols(g):
        inner = []
        for side, (device, has) in enumerate(sides):
            if g == 3:
                for which in range(2):
                    await_row(u, ur, ux_r, which, side)
            rows = jnp.concatenate([buf[i, :, HALVES[side]] for buf, i in groups[g]], axis=0)
            out = dot3(split(rows), (rcs[side, 0], rcs[side, 1]))
            halves = out[:, :BLOCK], out[:, BLOCK:]
            ts[g, side] = halves[side]
            inner.append(halves[1 - side])
            copy = remote(
                ts.at[g, side], tr.at[g, 1 - side],
                tx_s.at[g, side], tx_r.at[g, 1 - side], device,
            )
            side_copies.append((copy, has))

            @pl.when(has)
            def _():
                copy.start()

        flag = col_flag(1)
        tmid[g, :, :BLOCK] = pick(flag, inner[0], inner[1])
        tmid[g, :, BLOCK:] = pick(flag, inner[1], inner[0])

    def await_sides(g, outer, got, recv):
        for side, (device, has) in enumerate(sides):
            @pl.when(has)
            def _():
                arrived(got.at[g, side], recv.at[g, side])

            @pl.when(jnp.logical_not(has))
            def _():
                got[g, side] = outer[g, side]

    for t in range(2):
        y_begin(t)
    pieces_send()
    halo_send(0)
    across_send()
    y_first(0)
    y_first(1)
    z_begin(0)
    halo_send(3)
    y_second(0)
    z_first(0)
    z_begin(1)
    halo_send(1)
    y_second(1)
    z_first(1)
    y_third(0)
    halo_send(2)
    z_second(0)
    y_third(1)
    load.wait()
    mate_wait(0)
    split_rows(0)
    z_third(0)
    split_first()
    z_second(1)

    for k in (0, 3, 1, 2):
        first_cols(k)
        mix_rows(0, k, w[pl.ds(k * PAIR, PAIR), :], v)
        if k in (0, 3):
            for half in range(2):
                send_row(v, vr, vx_s, vx_r, k // 3, half)
    mate_wait(1)
    split_rows(1)
    second_rows(1)
    second_rows(2)
    for half in range(2):
        for which, k in ((0, 0), (1, 3)):
            await_row(v, vr, vx_r, which, half)
            second_rows(k, HALVES[half])
            send_row(u, ur, ux_s, ux_r, which, half)
    z_third(1)
    split_second()
    for g in range(4):
        second_cols(g)

    places = {1: (2, 0), 2: (0, 0), 3: (0, 1), 4: (1, 0), 5: (1, 1), 6: (2, 1), 0: (3, 0), 7: (3, 1)}
    finals = [row_flag(1, 0), row_flag(1, 1)]

    def parts(block):
        g, half = places[block]
        rows = pl.ds(half * BLOCK, BLOCK)
        return tr[g, 0, rows], tmid[g, rows], tr[g, 1, rows]

    outs = []

    def emit(position, flag, stay, other=None):
        rows = pl.ds(position * BLOCK, BLOCK)
        values = parts(stay)
        if other is not None:
            values = [pick(flag, a, b) for a, b in zip(values, parts(other))]
        obuf[rows, :BLOCK] = values[0]
        obuf[rows, BLOCK:3 * BLOCK] = values[1]
        obuf[rows, 3 * BLOCK:] = values[2]
        copy = pltpu.make_async_copy(obuf.at[rows], out_ref.at[rows], out_sem.at[position])
        copy.start()
        outs.append(copy)

    await_sides(0, ts, tr, tx_r)
    emit(4, None, 3)
    await_sides(1, ts, tr, tx_r)
    emit(3, None, 4)
    await_sides(2, ts, tr, tx_r)
    emit(1, finals[0], 1, 2)
    emit(2, finals[0], 2, 1)
    emit(5, finals[1], 5, 6)
    emit(6, finals[1], 6, 5)
    await_sides(3, ts, tr, tx_r)
    emit(0, None, 0)
    emit(7, None, 7)

    for copy in started:
        copy.wait_send()
    for h in range(2):
        there, here = across_copy(h)

        @pl.when(jnp.logical_not(stays[h]))
        def _():
            there.wait_send()

    for copy, has in row_copies + side_copies + piece_copies:
        @pl.when(has)
        def _():
            copy.wait_send()

    for copy in outs:
        copy.wait()


def body(covariance, rotations, pairing):
    dma = pltpu.SemaphoreType.DMA
    tile = covariance.shape
    wide = (BLOCK, tile[1])
    outer = pltpu.VMEM((4, 2, PAIR, BLOCK), F32)
    middle = pltpu.VMEM((4, PAIR, PAIR), F32)
    scratch = [
        pltpu.VMEM(tile, F32),
        pltpu.VMEM((2, tile[0], PAIR), F32),
        pltpu.VMEM((2, RP, Y, XH, CORE, 8, PAIR), F32),
        pltpu.VMEM((CB, XL, Z, 2, 8, BLOCK), F32),
        pltpu.VMEM((2, XL, Z, 2, 8, PAIR), F32),
        pltpu.VMEM((2, RP, 2, PAIR, PAIR), B16),
        pltpu.VMEM((CB, 2, PAIR, BLOCK), B16),
        pltpu.VMEM((2, 2, PAIR, PAIR), B16),
        pltpu.VMEM(tile, F32),
        pltpu.VMEM((RB, *wide), F32),
        pltpu.VMEM((2, *wide), F32),
        pltpu.VMEM((RB, *wide), F32),
        pltpu.VMEM((2, *wide), F32),
        outer, outer, middle,
        pltpu.VMEM(tile, F32),
        dma((3,)),
        dma((4, 2)), dma((4, 2)),
        dma((8,)), dma((CB, 2)),
        dma((2,)), dma((2,)),
        dma((2,)), dma((2,)),
        dma((2,)), dma((2,)),
        dma((2, 8)), dma((2, 8)),
        dma((2, 8)), dma((2, 8)),
        dma((2,)), dma((2,)),
        dma((2, 2)), dma((2, 2)),
        dma((2, 2)), dma((2, 2)),
        dma((4, 2)), dma((4, 2)),
        dma((RB,)),
    ]
    return pl.pallas_call(
        kernel,
        out_shape=jax.ShapeDtypeStruct(tile, F32),
        in_specs=[
            pl.BlockSpec(memory_space=pltpu.HBM),
            pl.BlockSpec(memory_space=pltpu.HBM),
            pl.BlockSpec(memory_space=pltpu.SMEM),
        ],
        out_specs=pl.BlockSpec(memory_space=pl.ANY),
        scratch_shapes=scratch,
        compiler_params=pltpu.CompilerParams(
            collective_id=0, has_side_effects=True, vmem_limit_bytes=60 * 2**20
        ),
        cost_estimate=pl.CostEstimate(
            flops=2 * 4 * tile[0] * tile[1] * PAIR, bytes_accessed=8 * tile[0] * tile[1],
            transcendentals=0,
        ),
    )(covariance, rotations, pairing)


def solution(mesh):
    in_specs = (P("row", "col"), P(None, "row", "col", None), P())
    out_specs = P("row", "col")
    return jax.shard_map(body, mesh=mesh, in_specs=in_specs, out_specs=out_specs, check_vma=False)
```

```python
import jax
import jax.numpy as jnp
from jax import lax
from jax.experimental import pallas as pl
from jax.experimental.pallas import tpu as pltpu
from jax.sharding import PartitionSpec as P

BLOCK = 128
PAIR = 2 * BLOCK
ROWS, COLS = 16, 32
XL, Z, Y, XH, CORE = 2, 8, 8, 2, 2
RB, CB = 8, 4
RP = RB // 2
MESH = pl.DeviceIdType.MESH
F32, B16 = jnp.float32, jnp.bfloat16


def split(value):
    high = value.astype(B16)
    low = (value - high.astype(F32)).astype(B16)
    return high, low


def dot(a, b):
    return jnp.dot(a, b, preferred_element_type=F32)


def dot3(a, b):
    return dot(a[0], b[0]) + (dot(a[0], b[1]) + dot(a[1], b[0]))


def kernel(
    cov_ref, rot_ref, pair_ref, out_ref,
    cbuf, halo, rr, rc0, rc, rrt, qs, rcs, w, v, vr, u, ur, ts, tr, tmid, obuf,
    loc_sem, h_s, h_r, t0_s, t0_r, tr_s, tr_r, xl_s, xl_r, xh_s, xh_r, z_s, z_r, y_s, y_r, mt_s, mt_r,
    vx_s, vx_r, ux_s, ux_r, tx_s, tx_r, out_sem,
):
    r = lax.axis_index("row")
    c = lax.axis_index("col")
    xl, z = r // Z, r % Z
    y, xh, core = c // 4, (c // 2) % 2, c % 2

    def z_dev(step):
        return (xl * Z + (z + step + Z) % Z, c)

    def y_dev(step):
        return (r, ((y + step + Y) % Y) * 4 + xh * 2 + core)

    mate = (r, y * 4 + xh * 2 + (1 - core))
    xh_mate = (r, y * 4 + (1 - xh) * 2 + core)
    xl_mate = ((1 - xl) * Z + z, c)
    up = ((r + ROWS - 1) % ROWS, c)
    down = ((r + 1) % ROWS, c)
    left = (r, (c + COLS - 1) % COLS)
    right = (r, (c + 1) % COLS)
    across = [(c // 2, 2 * r + h) for h in range(2)]
    diagonal = c // 2 == r
    stays = [jnp.logical_and(diagonal, core == h) for h in range(2)]
    ends = ((0, up, r > 0), (RB - 1, down, r < ROWS - 1))
    sides = ((left, c > 0), (right, c < COLS - 1))

    def remote(src, dst, send, recv, device):
        return pltpu.make_async_remote_copy(
            src_ref=src, dst_ref=dst, send_sem=send, recv_sem=recv,
            device_id=device, device_id_type=MESH,
        )

    started = []

    def go(copy):
        copy.start()
        started.append(copy)

    def arrived(ref, recv):
        remote(ref, ref, loc_sem.at[0], recv, mate).wait_recv()

    load = pltpu.make_async_copy(cov_ref, cbuf, loc_sem.at[0])
    load.start()
    own = [
        pltpu.make_async_copy(rot_ref.at[t], rr.at[t, :, y, xh, core], loc_sem.at[1 + t])
        for t in range(2)
    ]
    for t in range(2):
        own[t].start()

    barrier = pltpu.get_barrier_semaphore()
    peers = [mate, xh_mate, xl_mate, up, down, left, right]
    peers += [dev(step) for dev in (z_dev, y_dev) for step in (1, -1, 2, -2)]
    for peer in peers:
        pl.semaphore_signal(barrier, inc=1, device_id=peer, device_id_type=MESH)
    beside = c // 2 + jnp.where(core == 0, -1, 1)
    has_beside = jnp.logical_and(beside >= 0, beside < ROWS)
    for s in range(2):
        @pl.when(jnp.logical_not(jnp.logical_and(diagonal, core == s)))
        def _():
            pl.semaphore_signal(barrier, inc=1, device_id=(c // 2, 2 * r + s), device_id_type=MESH)

        @pl.when(has_beside)
        def _():
            pl.semaphore_signal(
                barrier, inc=1, device_id=((beside + ROWS) % ROWS, 2 * r + s), device_id_type=MESH
            )
    targets = 2 + jnp.where(r > 0, 1, 0) + jnp.where(r < ROWS - 1, 1, 0) - jnp.where(diagonal, 1, 0)
    pl.semaphore_wait(barrier, len(peers) + targets)

    def halo_send(k):
        rows = pl.ds(k * PAIR, PAIR)
        for side, (device, has) in enumerate(sides):
            src = cov_ref.at[rows, pl.ds(side * PAIR, PAIR)]
            copy = remote(src, halo.at[1 - side, rows], h_s.at[k, side], h_r.at[k, 1 - side], device)
            here = pltpu.make_async_copy(src, halo.at[side, rows], h_r.at[k, side])
            side_copies.append((copy, has))

            @pl.when(has)
            def _():
                copy.start()

            @pl.when(jnp.logical_not(has))
            def _():
                here.start()

    def halo_wait(k):
        for side in range(2):
            arrived(halo.at[side, pl.ds(k * PAIR, PAIR)], h_r.at[k, side])

    side_copies = []

    first_tile = jnp.where(r > 0, 2 * r - 1, 0)
    last_tile = jnp.where(r < ROWS - 1, 2 * r + 2, COLS - 1)
    pieces = (
        (0, 0, first_tile, jnp.where(r > 0, 3, 0)),
        (0, 1, 2 * r, 1), (1, 0, 2 * r, 2), (2, 0, 2 * r, 3),
        (1, 1, 2 * r + 1, 0), (2, 1, 2 * r + 1, 1), (3, 0, 2 * r + 1, 2),
        (3, 1, last_tile, jnp.where(r < ROWS - 1, 0, 3)),
    )
    piece_copies = []

    def pieces_send():
        for i, (k, half, tile, position) in enumerate(pieces):
            src = rot_ref.at[0, k, :, pl.ds(half * BLOCK, BLOCK)]
            dst = rc0.at[position, c // 2 // Z, c // 2 % Z, core]
            there = remote(src, dst, t0_s.at[i], t0_r.at[position, core], (c // 2, tile))
            here = pltpu.make_async_copy(src, dst, t0_r.at[position, core])
            away = jnp.logical_not(jnp.logical_and(diagonal, tile == c))
            piece_copies.append((there, away))

            @pl.when(away)
            def _():
                there.start()

            @pl.when(jnp.logical_not(away))
            def _():
                here.start()

    def across_copy(h):
        src = rot_ref.at[1, pl.ds(2 * h, 2)]
        dst = rc.at[:, c // 2 // Z, c // 2 % Z, core]
        there = remote(src, dst, tr_s.at[h], tr_r.at[core], across[h])
        here = pltpu.make_async_copy(src, dst, tr_r.at[core])
        return there, here

    def across_send():
        for h in range(2):
            there, here = across_copy(h)

            @pl.when(stays[h])
            def _():
                here.start()

            @pl.when(jnp.logical_not(stays[h]))
            def _():
                there.start()

    def y_block(t, origin, half=None):
        if half is None:
            return rr.at[t, :, origin, :, core]
        return rr.at[t, :, origin, half, core]

    def z_block(t, origin, half=None):
        if t == 0:
            return rc0.at[:, :, origin] if half is None else rc0.at[:, half, origin]
        return rc.at[:, :, origin] if half is None else rc.at[:, half, origin]

    STEPS = (1, -1, 2, -2, 3, -3)

    def first_level(block, t, me, send, recv, dev, src=None):
        ref = block(t, me)
        src = ref if src is None else src
        for i in (2, 3, 0, 1):
            go(remote(src, ref, send.at[t, i], recv.at[t, i], dev(STEPS[i])))

    def second_level(block, t, me, n, send, recv, dev, then=None):
        for i in (2, 3):
            way = 1 if i == 2 else -1
            origin = (me - 2 * way + n) % n
            ref = block(t, origin)
            arrived(ref, recv.at[t, i])
            part = block(t, origin, i - 2)
            go(remote(part, part, send.at[t, i + 4], recv.at[t, i + 4], dev(2 * way)))
            go(remote(ref, ref, send.at[t, i + 2], recv.at[t, i + 2], dev(way)))
            if then is not None:
                then(t, origin)
        for i in (0, 1):
            origin = (me - STEPS[i] + n) % n
            arrived(block(t, origin), recv.at[t, i])
            if then is not None:
                then(t, origin)

    def third_level(block, t, me, n, recv, then=None):
        for i in (4, 5):
            origin = (me - STEPS[i] + n) % n
            arrived(block(t, origin), recv.at[t, i])
            if then is not None:
                then(t, origin)
        origin = (me + n // 2) % n
        for half in range(2):
            arrived(block(t, origin, half), recv.at[t, 6 + half])
        if then is not None:
            then(t, origin)

    def y_begin(t):
        go(remote(rot_ref.at[t], rr.at[t, :, y, xh, core], xh_s.at[t], xh_r.at[t], xh_mate))

    def y_first(t):
        own[t].wait()
        arrived(rr.at[t, :, y, 1 - xh, core], xh_r.at[t])
        first_level(y_block, t, y, y_s, y_r, y_dev)

    def y_second(t):
        second_level(y_block, t, y, Y, y_s, y_r, y_dev)

    def y_third(t):
        third_level(y_block, t, y, Y, y_r)
        ref = rr.at[t, :, :, :, core]
        go(remote(ref, ref, mt_s.at[t], mt_r.at[t], mate))

    def mate_wait(t):
        arrived(rr.at[t, :, :, :, 1 - core], mt_r.at[t])

    def z_begin(t):
        for s in range(2):
            if t == 0:
                for position in range(CB):
                    arrived(rc0.at[position, xl, z, s], t0_r.at[position, s])
            else:
                arrived(rc.at[:, xl, z, s], tr_r.at[s])
        ref = rc0.at[:, xl, z] if t == 0 else rc.at[:, xl, z]
        go(remote(ref, ref, xl_s.at[t], xl_r.at[t], xl_mate))

    def z_first(t):
        buf = rc0 if t == 0 else rc
        arrived(buf.at[:, 1 - xl, z], xl_r.at[t])
        first_level(z_block, t, z, z_s, z_r, z_dev)

    def z_second(t):
        second_level(z_block, t, z, Z, z_s, z_r, z_dev)

    def z_third(t):
        third_level(z_block, t, z, Z, z_r)

    def split_first():
        for position in range(CB):
            high, low = split(rc0[position].reshape(PAIR, BLOCK))
            qs[position, 0] = high
            qs[position, 1] = low

    def split_second():
        for k in range(2):
            high, low = split(rc[k].reshape(PAIR, PAIR))
            rcs[k, 0] = high
            rcs[k, 1] = low

    def split_rows(t):
        def one(k, _):
            high, low = split(rr[t, k].reshape(PAIR, PAIR).T)
            rrt[t, k, 0] = high
            rrt[t, k, 1] = low
            return 0
        lax.fori_loop(0, RP, one, 0)

    def col_flag(t):
        return pair_ref[t, c * CB + 1] - (c * CB + 1)

    def row_flag(t, which):
        first = r * RB + 1 + 4 * which
        return pair_ref[t, first] - first

    def pick(flag, stay, other):
        return jnp.where(jnp.full(stay.shape, flag, jnp.int32) != 0, other, stay)

    def mix_rows(t, k, value, buf, cols=slice(None)):
        out = dot3((rrt[t, k, 0], rrt[t, k, 1]), split(value))
        buf[2 * k, :, cols] = out[:BLOCK]
        buf[2 * k + 1, :, cols] = out[BLOCK:]

    row_copies = []
    HALVES = [pl.ds(half * PAIR, PAIR) for half in range(2)]

    def send_row(buf, got, send, recv, which, half):
        edge, device, has = ends[which]
        copy = remote(
            buf.at[edge, :, HALVES[half]], got.at[1 - which, :, HALVES[half]],
            send.at[half, which], recv.at[half, 1 - which], device,
        )
        row_copies.append((copy, has))

        @pl.when(has)
        def _():
            copy.start()

    def await_row(buf, got, recv, which, half):
        edge, device, has = ends[which]
        cols = HALVES[half]

        @pl.when(has)
        def _():
            arrived(got.at[which, :, cols], recv.at[half, which])

        @pl.when(jnp.logical_not(has))
        def _():
            got[which, :, cols] = buf[edge, :, cols]

    flags = [row_flag(0, 0), row_flag(0, 1)]

    def second_rows(k, cols=slice(None)):
        if k == 0:
            pair = (vr[0, :, cols], pick(flags[0], v[1, :, cols], v[2, :, cols]))
        elif k == 1:
            pair = (pick(flags[0], v[2, :, cols], v[1, :, cols]), v[4, :, cols])
        elif k == 2:
            pair = (v[3, :, cols], pick(flags[1], v[5, :, cols], v[6, :, cols]))
        else:
            pair = (pick(flags[1], v[6, :, cols], v[5, :, cols]), vr[1, :, cols])
        mix_rows(1, k, jnp.concatenate(pair, axis=0), u, cols)

    def first_cols(k):
        rows = pl.ds(k * PAIR, PAIR)
        halo_wait(k)
        values = (halo[0, rows], cbuf[rows, :PAIR], cbuf[rows, PAIR:], halo[1, rows])
        out = [dot3(split(value), (qs[p, 0], qs[p, 1])) for p, value in enumerate(values)]
        flag = col_flag(0)
        w[rows, :BLOCK] = out[0]
        w[rows, BLOCK:2 * BLOCK] = pick(flag, out[1], out[2])
        w[rows, 2 * BLOCK:3 * BLOCK] = pick(flag, out[2], out[1])
        w[rows, 3 * BLOCK:] = out[3]

    groups = (((u, 2), (u, 3)), ((u, 4), (u, 5)), ((u, 1), (u, 6)), ((ur, 0), (ur, 1)))

    def second_cols(g):
        inner = []
        for side, (device, has) in enumerate(sides):
            if g == 3:
                for which in range(2):
                    await_row(u, ur, ux_r, which, side)
            rows = jnp.concatenate([buf[i, :, HALVES[side]] for buf, i in groups[g]], axis=0)
            out = dot3(split(rows), (rcs[side, 0], rcs[side, 1]))
            halves = out[:, :BLOCK], out[:, BLOCK:]
            ts[g, side] = halves[side]
            inner.append(halves[1 - side])
            copy = remote(
                ts.at[g, side], tr.at[g, 1 - side],
                tx_s.at[g, side], tx_r.at[g, 1 - side], device,
            )
            side_copies.append((copy, has))

            @pl.when(has)
            def _():
                copy.start()

        flag = col_flag(1)
        tmid[g, :, :BLOCK] = pick(flag, inner[0], inner[1])
        tmid[g, :, BLOCK:] = pick(flag, inner[1], inner[0])

    def await_sides(g, outer, got, recv):
        for side, (device, has) in enumerate(sides):
            @pl.when(has)
            def _():
                arrived(got.at[g, side], recv.at[g, side])

            @pl.when(jnp.logical_not(has))
            def _():
                got[g, side] = outer[g, side]

    for t in range(2):
        y_begin(t)
    pieces_send()
    halo_send(0)
    across_send()
    y_first(0)
    y_first(1)
    z_begin(0)
    halo_send(3)
    y_second(0)
    z_first(0)
    z_begin(1)
    halo_send(1)
    y_second(1)
    z_first(1)
    z_second(0)
    halo_send(2)
    y_third(0)
    y_third(1)
    load.wait()
    mate_wait(0)
    split_rows(0)
    z_third(0)
    split_first()
    z_second(1)

    for k in (0, 3, 1, 2):
        first_cols(k)
        mix_rows(0, k, w[pl.ds(k * PAIR, PAIR), :], v)
        if k in (0, 3):
            for half in range(2):
                send_row(v, vr, vx_s, vx_r, k // 3, half)
    mate_wait(1)
    split_rows(1)
    second_rows(1)
    second_rows(2)
    z_third(1)
    split_second()
    second_cols(0)
    second_cols(1)
    for half in range(2):
        for which, k in ((0, 0), (1, 3)):
            await_row(v, vr, vx_r, which, half)
            second_rows(k, HALVES[half])
            send_row(u, ur, ux_s, ux_r, which, half)
    second_cols(2)
    second_cols(3)

    places = {1: (2, 0), 2: (0, 0), 3: (0, 1), 4: (1, 0), 5: (1, 1), 6: (2, 1), 0: (3, 0), 7: (3, 1)}
    finals = [row_flag(1, 0), row_flag(1, 1)]

    def parts(block):
        g, half = places[block]
        rows = pl.ds(half * BLOCK, BLOCK)
        return tr[g, 0, rows], tmid[g, rows], tr[g, 1, rows]

    outs = []

    def emit(position, flag, stay, other=None):
        rows = pl.ds(position * BLOCK, BLOCK)
        values = parts(stay)
        if other is not None:
            values = [pick(flag, a, b) for a, b in zip(values, parts(other))]
        obuf[rows, :BLOCK] = values[0]
        obuf[rows, BLOCK:3 * BLOCK] = values[1]
        obuf[rows, 3 * BLOCK:] = values[2]
        copy = pltpu.make_async_copy(obuf.at[rows], out_ref.at[rows], out_sem.at[position])
        copy.start()
        outs.append(copy)

    await_sides(0, ts, tr, tx_r)
    emit(4, None, 3)
    await_sides(1, ts, tr, tx_r)
    emit(3, None, 4)
    await_sides(2, ts, tr, tx_r)
    emit(1, finals[0], 1, 2)
    emit(2, finals[0], 2, 1)
    emit(5, finals[1], 5, 6)
    emit(6, finals[1], 6, 5)
    await_sides(3, ts, tr, tx_r)
    emit(0, None, 0)
    emit(7, None, 7)

    for copy in started:
        copy.wait_send()
    for h in range(2):
        there, here = across_copy(h)

        @pl.when(jnp.logical_not(stays[h]))
        def _():
            there.wait_send()

    for copy, has in row_copies + side_copies + piece_copies:
        @pl.when(has)
        def _():
            copy.wait_send()

    for copy in outs:
        copy.wait()


def place(src_ref, out_ref, held, load_sem, store_sem):
    parts = [pl.ds(i * BLOCK, BLOCK) for i in range(RB)]
    loads = [
        pltpu.make_async_copy(src_ref.at[rows], held.at[rows], load_sem.at[i])
        for i, rows in enumerate(parts)
    ]
    stores = [
        pltpu.make_async_copy(held.at[rows], out_ref.at[rows], store_sem.at[i])
        for i, rows in enumerate(parts)
    ]
    for load in loads:
        load.start()
    for load, store in zip(loads, stores):
        load.wait()
        store.start()
    for store in stores:
        store.wait()


def body(covariance, rotations, pairing):
    dma = pltpu.SemaphoreType.DMA
    tile = covariance.shape
    wide = (BLOCK, tile[1])
    outer = pltpu.VMEM((4, 2, PAIR, BLOCK), F32)
    middle = pltpu.VMEM((4, PAIR, PAIR), F32)
    scratch = [
        pltpu.VMEM(tile, F32),
        pltpu.VMEM((2, tile[0], PAIR), F32),
        pltpu.VMEM((2, RP, Y, XH, CORE, 8, PAIR), F32),
        pltpu.VMEM((CB, XL, Z, 2, 8, BLOCK), F32),
        pltpu.VMEM((2, XL, Z, 2, 8, PAIR), F32),
        pltpu.VMEM((2, RP, 2, PAIR, PAIR), B16),
        pltpu.VMEM((CB, 2, PAIR, BLOCK), B16),
        pltpu.VMEM((2, 2, PAIR, PAIR), B16),
        pltpu.VMEM(tile, F32),
        pltpu.VMEM((RB, *wide), F32),
        pltpu.VMEM((2, *wide), F32),
        pltpu.VMEM((RB, *wide), F32),
        pltpu.VMEM((2, *wide), F32),
        outer, outer, middle,
        pltpu.VMEM(tile, F32),
        dma((3,)),
        dma((4, 2)), dma((4, 2)),
        dma((8,)), dma((CB, 2)),
        dma((2,)), dma((2,)),
        dma((2,)), dma((2,)),
        dma((2,)), dma((2,)),
        dma((2, 8)), dma((2, 8)),
        dma((2, 8)), dma((2, 8)),
        dma((2,)), dma((2,)),
        dma((2, 2)), dma((2, 2)),
        dma((2, 2)), dma((2, 2)),
        dma((4, 2)), dma((4, 2)),
        dma((RB,)),
    ]
    mixed = pl.pallas_call(
        kernel,
        out_shape=jax.ShapeDtypeStruct(tile, F32),
        in_specs=[
            pl.BlockSpec(memory_space=pltpu.HBM),
            pl.BlockSpec(memory_space=pltpu.HBM),
            pl.BlockSpec(memory_space=pltpu.SMEM),
        ],
        out_specs=pl.BlockSpec(memory_space=pl.ANY),
        scratch_shapes=scratch,
        compiler_params=pltpu.CompilerParams(
            collective_id=0, has_side_effects=True, vmem_limit_bytes=60 * 2**20
        ),
        cost_estimate=pl.CostEstimate(
            flops=2 * 4 * tile[0] * tile[1] * PAIR, bytes_accessed=8 * tile[0] * tile[1],
            transcendentals=0,
        ),
    )(covariance, rotations, pairing)
    return pl.pallas_call(
        place,
        out_shape=jax.ShapeDtypeStruct(tile, F32),
        in_specs=[pl.BlockSpec(memory_space=pl.ANY)],
        out_specs=pl.BlockSpec(memory_space=pl.ANY),
        scratch_shapes=[
            pltpu.VMEM(tile, F32), pltpu.SemaphoreType.DMA((RB,)), pltpu.SemaphoreType.DMA((RB,))
        ],
        compiler_params=pltpu.CompilerParams(vmem_limit_bytes=60 * 2**20),
    )(mixed)


def solution(mesh):
    in_specs = (P("row", "col"), P(None, "row", "col", None), P())
    out_specs = P("row", "col")
    return jax.shard_map(body, mesh=mesh, in_specs=in_specs, out_specs=out_specs, check_vma=False)
```

```python
import jax
import jax.numpy as jnp
from jax import lax
from jax.experimental import pallas as pl
from jax.experimental.pallas import tpu as pltpu
from jax.sharding import PartitionSpec as P

BLOCK = 128
PAIR = 2 * BLOCK
ROWS, COLS = 16, 32
XL, Z, Y, XH, CORE = 2, 8, 8, 2, 2
RB, CB = 8, 4
RP = RB // 2
PARTS = 4
MESH = pl.DeviceIdType.MESH
F32, B16 = jnp.float32, jnp.bfloat16


def split(value):
    high = value.astype(B16)
    low = (value - high.astype(F32)).astype(B16)
    return high, low


def dot(a, b):
    return jnp.dot(a, b, preferred_element_type=F32)


def dot3(a, b):
    return dot(a[0], b[0]) + (dot(a[0], b[1]) + dot(a[1], b[0]))


def kernel(
    cov_ref, rot_ref, pair_ref, out_ref,
    cbuf, halo, rr, rc0, rc, rrt, qs, rcs, w, v, vr, u, ur, ts, tr, tmid, obuf,
    loc_sem, h_s, h_r, t0_s, t0_r, tr_s, tr_r, xl_s, xl_r, xh_s, xh_r, z_s, z_r, y_s, y_r, mt_s, mt_r,
    vx_s, vx_r, ux_s, ux_r, tx_s, tx_r, out_sem,
):
    r = lax.axis_index("row")
    c = lax.axis_index("col")
    xl, z = r // Z, r % Z
    y, xh, core = c // 4, (c // 2) % 2, c % 2

    def z_dev(step):
        return (xl * Z + (z + step + Z) % Z, c)

    def y_dev(step):
        return (r, ((y + step + Y) % Y) * 4 + xh * 2 + core)

    mate = (r, y * 4 + xh * 2 + (1 - core))
    xh_mate = (r, y * 4 + (1 - xh) * 2 + core)
    xl_mate = ((1 - xl) * Z + z, c)
    up = ((r + ROWS - 1) % ROWS, c)
    down = ((r + 1) % ROWS, c)
    left = (r, (c + COLS - 1) % COLS)
    right = (r, (c + 1) % COLS)
    across = [(c // 2, 2 * r + h) for h in range(2)]
    diagonal = c // 2 == r
    stays = [jnp.logical_and(diagonal, core == h) for h in range(2)]
    ends = ((0, up, r > 0), (RB - 1, down, r < ROWS - 1))
    sides = ((left, c > 0), (right, c < COLS - 1))

    def remote(src, dst, send, recv, device):
        return pltpu.make_async_remote_copy(
            src_ref=src, dst_ref=dst, send_sem=send, recv_sem=recv,
            device_id=device, device_id_type=MESH,
        )

    started = []

    def go(copy):
        copy.start()
        started.append(copy)

    def arrived(ref, recv):
        remote(ref, ref, loc_sem.at[0], recv, mate).wait_recv()

    load = pltpu.make_async_copy(cov_ref, cbuf, loc_sem.at[0])
    load.start()
    own = [
        pltpu.make_async_copy(rot_ref.at[t], rr.at[t, :, y, xh, core], loc_sem.at[1 + t])
        for t in range(2)
    ]
    for t in range(2):
        own[t].start()

    barrier = pltpu.get_barrier_semaphore()
    peers = [mate, xh_mate, xl_mate, up, down, left, right]
    peers += [dev(step) for dev in (z_dev, y_dev) for step in (1, -1, 2, -2)]
    for peer in peers:
        pl.semaphore_signal(barrier, inc=1, device_id=peer, device_id_type=MESH)
    beside = c // 2 + jnp.where(core == 0, -1, 1)
    has_beside = jnp.logical_and(beside >= 0, beside < ROWS)
    for s in range(2):
        @pl.when(jnp.logical_not(jnp.logical_and(diagonal, core == s)))
        def _():
            pl.semaphore_signal(barrier, inc=1, device_id=(c // 2, 2 * r + s), device_id_type=MESH)

        @pl.when(has_beside)
        def _():
            pl.semaphore_signal(
                barrier, inc=1, device_id=((beside + ROWS) % ROWS, 2 * r + s), device_id_type=MESH
            )
    targets = 2 + jnp.where(r > 0, 1, 0) + jnp.where(r < ROWS - 1, 1, 0) - jnp.where(diagonal, 1, 0)
    pl.semaphore_wait(barrier, len(peers) + targets)

    def halo_send(k):
        rows = pl.ds(k * PAIR, PAIR)
        for side, (device, has) in enumerate(sides):
            src = cov_ref.at[rows, pl.ds(side * PAIR, PAIR)]
            copy = remote(src, halo.at[1 - side, rows], h_s.at[k, side], h_r.at[k, 1 - side], device)
            here = pltpu.make_async_copy(src, halo.at[side, rows], h_r.at[k, side])
            side_copies.append((copy, has))

            @pl.when(has)
            def _():
                copy.start()

            @pl.when(jnp.logical_not(has))
            def _():
                here.start()

    def halo_wait(k):
        for side in range(2):
            arrived(halo.at[side, pl.ds(k * PAIR, PAIR)], h_r.at[k, side])

    side_copies = []

    first_tile = jnp.where(r > 0, 2 * r - 1, 0)
    last_tile = jnp.where(r < ROWS - 1, 2 * r + 2, COLS - 1)
    pieces = (
        (0, 0, first_tile, jnp.where(r > 0, 3, 0)),
        (0, 1, 2 * r, 1), (1, 0, 2 * r, 2), (2, 0, 2 * r, 3),
        (1, 1, 2 * r + 1, 0), (2, 1, 2 * r + 1, 1), (3, 0, 2 * r + 1, 2),
        (3, 1, last_tile, jnp.where(r < ROWS - 1, 0, 3)),
    )
    piece_copies = []

    def pieces_send():
        for i, (k, half, tile, position) in enumerate(pieces):
            src = rot_ref.at[0, k, :, pl.ds(half * BLOCK, BLOCK)]
            dst = rc0.at[position, c // 2 // Z, c // 2 % Z, core]
            there = remote(src, dst, t0_s.at[i], t0_r.at[position, core], (c // 2, tile))
            here = pltpu.make_async_copy(src, dst, t0_r.at[position, core])
            away = jnp.logical_not(jnp.logical_and(diagonal, tile == c))
            piece_copies.append((there, away))

            @pl.when(away)
            def _():
                there.start()

            @pl.when(jnp.logical_not(away))
            def _():
                here.start()

    def across_copy(h):
        src = rot_ref.at[1, pl.ds(2 * h, 2)]
        dst = rc.at[:, c // 2 // Z, c // 2 % Z, core]
        there = remote(src, dst, tr_s.at[h], tr_r.at[core], across[h])
        here = pltpu.make_async_copy(src, dst, tr_r.at[core])
        return there, here

    def across_send():
        for h in range(2):
            there, here = across_copy(h)

            @pl.when(stays[h])
            def _():
                here.start()

            @pl.when(jnp.logical_not(stays[h]))
            def _():
                there.start()

    def y_block(t, origin, half=None):
        if half is None:
            return rr.at[t, :, origin, :, core]
        return rr.at[t, :, origin, half, core]

    def z_block(t, origin, half=None):
        if t == 0:
            return rc0.at[:, :, origin] if half is None else rc0.at[:, half, origin]
        return rc.at[:, :, origin] if half is None else rc.at[:, half, origin]

    STEPS = (1, -1, 2, -2, 3, -3)

    def first_level(block, t, me, send, recv, dev, src=None):
        ref = block(t, me)
        src = ref if src is None else src
        for i in (2, 3, 0, 1):
            go(remote(src, ref, send.at[t, i], recv.at[t, i], dev(STEPS[i])))

    def second_level(block, t, me, n, send, recv, dev, then=None):
        for i in (2, 3):
            way = 1 if i == 2 else -1
            origin = (me - 2 * way + n) % n
            ref = block(t, origin)
            arrived(ref, recv.at[t, i])
            part = block(t, origin, i - 2)
            go(remote(part, part, send.at[t, i + 4], recv.at[t, i + 4], dev(2 * way)))
            go(remote(ref, ref, send.at[t, i + 2], recv.at[t, i + 2], dev(way)))
            if then is not None:
                then(t, origin)
        for i in (0, 1):
            origin = (me - STEPS[i] + n) % n
            arrived(block(t, origin), recv.at[t, i])
            if then is not None:
                then(t, origin)

    def third_level(block, t, me, n, recv, then=None):
        for i in (4, 5):
            origin = (me - STEPS[i] + n) % n
            arrived(block(t, origin), recv.at[t, i])
            if then is not None:
                then(t, origin)
        origin = (me + n // 2) % n
        for half in range(2):
            arrived(block(t, origin, half), recv.at[t, 6 + half])
        if then is not None:
            then(t, origin)

    def y_begin(t):
        go(remote(rot_ref.at[t], rr.at[t, :, y, xh, core], xh_s.at[t], xh_r.at[t], xh_mate))

    def y_first(t):
        own[t].wait()
        arrived(rr.at[t, :, y, 1 - xh, core], xh_r.at[t])
        first_level(y_block, t, y, y_s, y_r, y_dev)

    def y_second(t):
        second_level(y_block, t, y, Y, y_s, y_r, y_dev)

    def y_third(t):
        third_level(y_block, t, y, Y, y_r)
        ref = rr.at[t, :, :, :, core]
        go(remote(ref, ref, mt_s.at[t], mt_r.at[t], mate))

    def mate_wait(t):
        arrived(rr.at[t, :, :, :, 1 - core], mt_r.at[t])

    def z_begin(t):
        for s in range(2):
            if t == 0:
                for position in range(CB):
                    arrived(rc0.at[position, xl, z, s], t0_r.at[position, s])
            else:
                arrived(rc.at[:, xl, z, s], tr_r.at[s])
        ref = rc0.at[:, xl, z] if t == 0 else rc.at[:, xl, z]
        go(remote(ref, ref, xl_s.at[t], xl_r.at[t], xl_mate))

    def z_first(t):
        buf = rc0 if t == 0 else rc
        arrived(buf.at[:, 1 - xl, z], xl_r.at[t])
        first_level(z_block, t, z, z_s, z_r, z_dev)

    def z_second(t):
        second_level(z_block, t, z, Z, z_s, z_r, z_dev)

    def z_third(t):
        third_level(z_block, t, z, Z, z_r)

    def split_first():
        for position in range(CB):
            high, low = split(rc0[position].reshape(PAIR, BLOCK))
            qs[position, 0] = high
            qs[position, 1] = low

    def split_second():
        for k in range(2):
            high, low = split(rc[k].reshape(PAIR, PAIR))
            rcs[k, 0] = high
            rcs[k, 1] = low

    def split_rows(t):
        def one(k, _):
            high, low = split(rr[t, k].reshape(PAIR, PAIR).T)
            rrt[t, k, 0] = high
            rrt[t, k, 1] = low
            return 0
        lax.fori_loop(0, RP, one, 0)

    def col_flag(t):
        return pair_ref[t, c * CB + 1] - (c * CB + 1)

    def row_flag(t, which):
        first = r * RB + 1 + 4 * which
        return pair_ref[t, first] - first

    def pick(flag, stay, other):
        return jnp.where(jnp.full(stay.shape, flag, jnp.int32) != 0, other, stay)

    def mix_rows(t, k, value, buf, cols=slice(None)):
        out = dot3((rrt[t, k, 0], rrt[t, k, 1]), split(value))
        buf[2 * k, :, cols] = out[:BLOCK]
        buf[2 * k + 1, :, cols] = out[BLOCK:]

    row_copies = []
    HALVES = [pl.ds(half * PAIR, PAIR) for half in range(2)]

    def send_row(buf, got, send, recv, which, half):
        edge, device, has = ends[which]
        copy = remote(
            buf.at[edge, :, HALVES[half]], got.at[1 - which, :, HALVES[half]],
            send.at[half, which], recv.at[half, 1 - which], device,
        )
        row_copies.append((copy, has))

        @pl.when(has)
        def _():
            copy.start()

    def await_row(buf, got, recv, which, half):
        edge, device, has = ends[which]
        cols = HALVES[half]

        @pl.when(has)
        def _():
            arrived(got.at[which, :, cols], recv.at[half, which])

        @pl.when(jnp.logical_not(has))
        def _():
            got[which, :, cols] = buf[edge, :, cols]

    flags = [row_flag(0, 0), row_flag(0, 1)]

    def second_rows(k, cols=slice(None)):
        if k == 0:
            pair = (vr[0, :, cols], pick(flags[0], v[1, :, cols], v[2, :, cols]))
        elif k == 1:
            pair = (pick(flags[0], v[2, :, cols], v[1, :, cols]), v[4, :, cols])
        elif k == 2:
            pair = (v[3, :, cols], pick(flags[1], v[5, :, cols], v[6, :, cols]))
        else:
            pair = (pick(flags[1], v[6, :, cols], v[5, :, cols]), vr[1, :, cols])
        mix_rows(1, k, jnp.concatenate(pair, axis=0), u, cols)

    def first_cols(k):
        rows = pl.ds(k * PAIR, PAIR)
        halo_wait(k)
        values = (halo[0, rows], cbuf[rows, :PAIR], cbuf[rows, PAIR:], halo[1, rows])
        out = [dot3(split(value), (qs[p, 0], qs[p, 1])) for p, value in enumerate(values)]
        flag = col_flag(0)
        w[rows, :BLOCK] = out[0]
        w[rows, BLOCK:2 * BLOCK] = pick(flag, out[1], out[2])
        w[rows, 2 * BLOCK:3 * BLOCK] = pick(flag, out[2], out[1])
        w[rows, 3 * BLOCK:] = out[3]

    groups = (((u, 2), (u, 3)), ((u, 4), (u, 5)), ((u, 1), (u, 6)), ((ur, 0), (ur, 1)))

    def second_cols(g):
        inner = []
        for side, (device, has) in enumerate(sides):
            if g == 3:
                for which in range(2):
                    await_row(u, ur, ux_r, which, side)
            rows = jnp.concatenate([buf[i, :, HALVES[side]] for buf, i in groups[g]], axis=0)
            out = dot3(split(rows), (rcs[side, 0], rcs[side, 1]))
            halves = out[:, :BLOCK], out[:, BLOCK:]
            ts[g, side] = halves[side]
            inner.append(halves[1 - side])
            copy = remote(
                ts.at[g, side], tr.at[g, 1 - side],
                tx_s.at[g, side], tx_r.at[g, 1 - side], device,
            )
            side_copies.append((copy, has))

            @pl.when(has)
            def _():
                copy.start()

        flag = col_flag(1)
        tmid[g, :, :BLOCK] = pick(flag, inner[0], inner[1])
        tmid[g, :, BLOCK:] = pick(flag, inner[1], inner[0])

    def await_sides(g, outer, got, recv):
        for side, (device, has) in enumerate(sides):
            @pl.when(has)
            def _():
                arrived(got.at[g, side], recv.at[g, side])

            @pl.when(jnp.logical_not(has))
            def _():
                got[g, side] = outer[g, side]

    for t in range(2):
        y_begin(t)
    pieces_send()
    halo_send(0)
    across_send()
    y_first(0)
    y_first(1)
    z_begin(0)
    halo_send(3)
    y_second(0)
    z_first(0)
    z_begin(1)
    halo_send(1)
    y_second(1)
    z_first(1)
    z_second(0)
    halo_send(2)
    y_third(0)
    y_third(1)
    load.wait()
    mate_wait(0)
    split_rows(0)
    z_third(0)
    split_first()
    z_second(1)

    for k in (0, 3, 1, 2):
        first_cols(k)
        mix_rows(0, k, w[pl.ds(k * PAIR, PAIR), :], v)
        if k in (0, 3):
            for half in range(2):
                send_row(v, vr, vx_s, vx_r, k // 3, half)
    mate_wait(1)
    split_rows(1)
    second_rows(1)
    second_rows(2)
    z_third(1)
    split_second()
    second_cols(0)
    second_cols(1)
    for half in range(2):
        for which, k in ((0, 0), (1, 3)):
            await_row(v, vr, vx_r, which, half)
            second_rows(k, HALVES[half])
            send_row(u, ur, ux_s, ux_r, which, half)
    second_cols(2)
    second_cols(3)

    places = {1: (2, 0), 2: (0, 0), 3: (0, 1), 4: (1, 0), 5: (1, 1), 6: (2, 1), 0: (3, 0), 7: (3, 1)}
    finals = [row_flag(1, 0), row_flag(1, 1)]

    def parts(block):
        g, half = places[block]
        rows = pl.ds(half * BLOCK, BLOCK)
        return tr[g, 0, rows], tmid[g, rows], tr[g, 1, rows]

    outs = []

    def emit(position, flag, stay, other=None):
        rows = pl.ds(position * BLOCK, BLOCK)
        values = parts(stay)
        if other is not None:
            values = [pick(flag, a, b) for a, b in zip(values, parts(other))]
        obuf[rows, :BLOCK] = values[0]
        obuf[rows, BLOCK:3 * BLOCK] = values[1]
        obuf[rows, 3 * BLOCK:] = values[2]
        copy = pltpu.make_async_copy(obuf.at[rows], out_ref.at[rows], out_sem.at[position])
        copy.start()
        outs.append(copy)

    await_sides(0, ts, tr, tx_r)
    emit(4, None, 3)
    await_sides(1, ts, tr, tx_r)
    emit(3, None, 4)
    await_sides(2, ts, tr, tx_r)
    emit(1, finals[0], 1, 2)
    emit(2, finals[0], 2, 1)
    emit(5, finals[1], 5, 6)
    emit(6, finals[1], 6, 5)
    await_sides(3, ts, tr, tx_r)
    emit(0, None, 0)
    emit(7, None, 7)

    for copy in started:
        copy.wait_send()
    for h in range(2):
        there, here = across_copy(h)

        @pl.when(jnp.logical_not(stays[h]))
        def _():
            there.wait_send()

    for copy, has in row_copies + side_copies + piece_copies:
        @pl.when(has)
        def _():
            copy.wait_send()

    for copy in outs:
        copy.wait()


def place(src_ref, out_ref, held, load_sem, store_sem):
    rows_each = src_ref.shape[0] // PARTS
    parts = [pl.ds(i * rows_each, rows_each) for i in range(PARTS)]
    loads = [
        pltpu.make_async_copy(src_ref.at[rows], held.at[rows], load_sem.at[i])
        for i, rows in enumerate(parts)
    ]
    stores = [
        pltpu.make_async_copy(held.at[rows], out_ref.at[rows], store_sem.at[i])
        for i, rows in enumerate(parts)
    ]
    for load in loads:
        load.start()
    for load, store in zip(loads, stores):
        load.wait()
        store.start()
    for store in stores:
        store.wait()


def body(covariance, rotations, pairing):
    dma = pltpu.SemaphoreType.DMA
    tile = covariance.shape
    wide = (BLOCK, tile[1])
    outer = pltpu.VMEM((4, 2, PAIR, BLOCK), F32)
    middle = pltpu.VMEM((4, PAIR, PAIR), F32)
    scratch = [
        pltpu.VMEM(tile, F32),
        pltpu.VMEM((2, tile[0], PAIR), F32),
        pltpu.VMEM((2, RP, Y, XH, CORE, 8, PAIR), F32),
        pltpu.VMEM((CB, XL, Z, 2, 8, BLOCK), F32),
        pltpu.VMEM((2, XL, Z, 2, 8, PAIR), F32),
        pltpu.VMEM((2, RP, 2, PAIR, PAIR), B16),
        pltpu.VMEM((CB, 2, PAIR, BLOCK), B16),
        pltpu.VMEM((2, 2, PAIR, PAIR), B16),
        pltpu.VMEM(tile, F32),
        pltpu.VMEM((RB, *wide), F32),
        pltpu.VMEM((2, *wide), F32),
        pltpu.VMEM((RB, *wide), F32),
        pltpu.VMEM((2, *wide), F32),
        outer, outer, middle,
        pltpu.VMEM(tile, F32),
        dma((3,)),
        dma((4, 2)), dma((4, 2)),
        dma((8,)), dma((CB, 2)),
        dma((2,)), dma((2,)),
        dma((2,)), dma((2,)),
        dma((2,)), dma((2,)),
        dma((2, 8)), dma((2, 8)),
        dma((2, 8)), dma((2, 8)),
        dma((2,)), dma((2,)),
        dma((2, 2)), dma((2, 2)),
        dma((2, 2)), dma((2, 2)),
        dma((4, 2)), dma((4, 2)),
        dma((RB,)),
    ]
    mixed = pl.pallas_call(
        kernel,
        out_shape=jax.ShapeDtypeStruct(tile, F32),
        in_specs=[
            pl.BlockSpec(memory_space=pltpu.HBM),
            pl.BlockSpec(memory_space=pltpu.HBM),
            pl.BlockSpec(memory_space=pltpu.SMEM),
        ],
        out_specs=pl.BlockSpec(memory_space=pl.ANY),
        scratch_shapes=scratch,
        compiler_params=pltpu.CompilerParams(
            collective_id=0, has_side_effects=True, vmem_limit_bytes=60 * 2**20
        ),
        cost_estimate=pl.CostEstimate(
            flops=2 * 4 * tile[0] * tile[1] * PAIR, bytes_accessed=8 * tile[0] * tile[1],
            transcendentals=0,
        ),
    )(covariance, rotations, pairing)
    return pl.pallas_call(
        place,
        out_shape=jax.ShapeDtypeStruct(tile, F32),
        in_specs=[pl.BlockSpec(memory_space=pl.ANY)],
        out_specs=pl.BlockSpec(memory_space=pl.ANY),
        scratch_shapes=[
            pltpu.VMEM(tile, F32), pltpu.SemaphoreType.DMA((PARTS,)), pltpu.SemaphoreType.DMA((PARTS,))
        ],
        compiler_params=pltpu.CompilerParams(vmem_limit_bytes=60 * 2**20),
    )(mixed)


def solution(mesh):
    in_specs = (P("row", "col"), P(None, "row", "col", None), P())
    out_specs = P("row", "col")
    return jax.shard_map(body, mesh=mesh, in_specs=in_specs, out_specs=out_specs, check_vma=False)
```
